512 devices in a mesh: seq: 128 (over z, x, y_lo, core), loc: 4 (over y_hi).
Axes of the slice: x: 4, y: 8 (y_hi: 4, y_lo: 2; y = y_hi * 2 + y_lo), z: 8, core: 2. Of those that a mesh axis runs over, the one named last changes fastest.
Arguments:
- queries: bfloat16 [3840, 4096], P('seq', 'loc'), may hold values from -32 to 32
- keys: bfloat16 [3840, 4096], P('seq', 'loc'), may hold values from -32 to 32
- values: bfloat16 [3840, 4096], P('seq', 'loc'), may hold values from -6 to 6
- positions: int32 [3840], P('seq'), may hold values from 0 to 3839, as said below
- byte_embed: bfloat16 [30720, 1024], P('seq', 'loc'), may hold values from -6 to 6
- w_slot: bfloat16 [512, 1024], replicated, may hold values from -0.25 to 0.25
- gain: float32 [1024], P('loc'), may hold values from 0.1 to 1.9
Outputs:
- local_input: bfloat16 [30720, 1024], P('seq', 'loc')
The draws below stay inside these ranges and needn't reach their ends.
Inputs may be any that keep to these rules, and one draw needn't show every extreme that they name: positions is a permutation of the patch positions; each aligned run of 15 rows holds consecutive ascending positions.
All inputs are finite; a program needn't handle non-finite values.
Results may differ from the reference program's by a relative error of at most 0.0065.
Values may be sent and summed in bfloat16 or wider, within the bound.
No kernel may reach another device: no remote copies, remote signals or barrier semaphores. Data moves between devices by JAX's collectives and lax.ppermute only.
A program may use at most 128 MiB of HBM per device.

```python
import math
import jax
import jax.numpy as jnp
from jax import lax

HEADS = 32
HEAD_DIM = 128
PATCH = 8
LOCAL_D = 1024
RUN = 15
D_G = 4096
SLOT_D = 512
PATCHES = 3840
BYTES = 30720


def draw_queries(key, part):
    key = jax.random.fold_in(key, 11)
    drawn = jax.random.normal(key, (PATCHES, HEADS * HEAD_DIM), jnp.float32)
    return drawn.astype(jnp.bfloat16)


def draw_keys(key, part):
    key = jax.random.fold_in(key, 23)
    drawn = jax.random.normal(key, (PATCHES, HEADS * HEAD_DIM), jnp.float32)
    return drawn.astype(jnp.bfloat16)


def draw_positions(key, part):
    key = jax.random.fold_in(key, 37)
    run_count = PATCHES // RUN
    order = jax.random.permutation(key, run_count).astype(jnp.int32)
    row_index = jnp.arange(PATCHES, dtype=jnp.int32)
    return order[row_index // RUN] * RUN + row_index % RUN


def block_scale(own_key, shape, cuts, smallest, high):
    loudness, own = 1.0, jax.random.fold_in(own_key, 6)
    for position, blocks in cuts:
        heights = jnp.exp(jax.random.uniform(jax.random.fold_in(own, position), (blocks,), jnp.float32, smallest / len(cuts), high / len(cuts)))
        loudness = loudness * jnp.repeat(heights, shape[position] // blocks).reshape([-1 if axis == position else 1 for axis in range(len(shape))])
    return loudness


def bell_draw(rng, extent, deviation, limit, cuts=(), held_as=jnp.bfloat16):
    result = deviation * jax.random.normal(rng, extent, jnp.float32)
    if cuts:
        result = result * block_scale(rng, extent, cuts, -0.22, 0.18)
    return jnp.clip(result, -limit, limit).astype(held_as)


def setup_inputs(seed: int = 0) -> dict:
    key_of = jax.random.split(jax.random.key(seed), 8)
    queries = draw_queries(jax.random.fold_in(key_of[7], 71), 0)
    keys = draw_keys(jax.random.fold_in(key_of[7], 71), 0)
    values = bell_draw(key_of[2], (PATCHES, D_G), 1.0, 6.0, ((0, 128), (1, 4)))
    positions = draw_positions(jax.random.fold_in(key_of[7], 71), 0)
    byte_embed = bell_draw(key_of[4], (BYTES, LOCAL_D), 1.0, 6.0, ((0, 128), (1, 4)))
    w_slot = bell_draw(key_of[5], (SLOT_D, LOCAL_D), SLOT_D ** -0.5, 0.25)
    gain = jnp.clip(1.0 + 0.18 * jax.random.normal(key_of[6], (LOCAL_D,), jnp.float32), 0.1, 1.9)
    return {"queries": queries, "keys": keys, "values": values, "positions": positions, "byte_embed": byte_embed, "w_slot": w_slot, "gain": gain}


def reference(queries, keys, values, positions, byte_embed, w_slot, gain):
    count = queries.shape[0]
    scale = 1.0 / math.sqrt(HEAD_DIM)
    query_heads = queries.reshape(count, HEADS, HEAD_DIM).astype(jnp.float32)
    key_heads = keys.reshape(count, HEADS, HEAD_DIM).astype(jnp.float32)
    value_heads = values.reshape(count, HEADS, HEAD_DIM).astype(jnp.float32)
    scores = jnp.einsum('qhd,khd->hqk', query_heads, key_heads) * scale
    allowed = (positions[None, :] <= positions[:, None])[None, :, :]
    masked = jnp.where(allowed, scores, jnp.float32(-1e+30))
    highest = lax.optimization_barrier(jnp.max(masked, axis=-1, keepdims=True))
    weights = jnp.where(allowed, jnp.exp(scores - highest), jnp.float32(0.0))
    denom = lax.optimization_barrier(jnp.sum(weights, axis=-1))
    summed = jnp.einsum('hqk,khd->hqd', weights, value_heads) / denom[:, :, None]
    attended = jnp.transpose(summed, (1, 0, 2)).reshape(count, HEADS * HEAD_DIM).astype(jnp.bfloat16)
    slots = attended.reshape(count * PATCH, SLOT_D)
    mixed = jnp.dot(slots, w_slot, preferred_element_type=jnp.float32) + byte_embed.astype(jnp.float32)
    spread = lax.optimization_barrier(jnp.mean(mixed * mixed, axis=-1, keepdims=True)) + 1e-05
    return (mixed / jnp.sqrt(spread) * gain[None, :]).astype(jnp.bfloat16)
```

```python
import math

import jax
import jax.numpy as jnp
from jax import lax
from jax.experimental import pallas as pl
from jax.experimental.pallas import tpu as pltpu
from jax.sharding import Mesh
from jax.sharding import PartitionSpec as P

HEAD_DIM = 128
PATCH = 8
RUN = 15
RUNS = 2
ROWS = RUN * RUNS
TILE = 16
PAD = RUNS * TILE
CHUNK = 8
CHUNKS = 4
HEADS_HERE = 8
LOCAL_D = 1024
SLOT_D = 512
LOCS = 4
COLS = LOCAL_D // LOCS
SEQ = ("za", "zb", "zc", "x", "yl", "c")
GROUP = ("za", "zb", "zc", "x", "yl")
PEERS = RUNS * CHUNKS * HEADS_HERE
QN = PEERS * TILE
KN = PEERS * CHUNK
STEP = 256
FLOOR = -1e20
MASKED = -1e30
FAR = 1e6
bf16 = jnp.bfloat16
f32 = jnp.float32


def iota(shape, dim):
    return lax.broadcasted_iota(jnp.int32, shape, dim)


def pick(condition, rows):
    select = jnp.where(condition, f32(1), f32(0)).astype(bf16)
    return jnp.dot(select, rows, preferred_element_type=f32)


def three_parts(x):
    high = x.astype(bf16).astype(f32)
    middle = (x - high).astype(bf16).astype(f32)
    return high, middle, x - high - middle


def pack(
    pos_hbm, q_hbm, k_hbm, v_hbm, e_hbm, gain_hbm, out_ref, e_out, pos_ref, q_ref, k_ref, v_ref, e_ref, gain_ref, sems
):
    pairs = [
        (pos_hbm, pos_ref),
        (q_hbm, q_ref),
        (k_hbm, k_ref),
        (v_hbm, v_ref),
        (e_hbm, e_ref),
        (gain_hbm, gain_ref),
    ]
    copies = [pltpu.make_async_copy(a, b, sems.at[n]) for n, (a, b) in enumerate(pairs)]
    for copy in copies:
        copy.start()
    for copy in copies[:2]:
        copy.wait()

    wide = (PAD, HEADS_HERE * HEAD_DIM)
    to, source = iota((PAD, ROWS), 0), iota((PAD, ROWS), 1)
    place = to % TILE
    queries = pick((source == to // TILE * RUN + place) & (place < RUN), q_ref[...])
    first = (pos_ref[0] // RUN).astype(f32)
    second = (pos_ref[RUN] // RUN).astype(f32)
    numbers = jnp.where(iota(wide, 1) % HEAD_DIM < HEAD_DIM // 2, first, second)
    queries = jnp.where(iota(wide, 0) % TILE == RUN, numbers, queries).astype(bf16)

    for copy in copies[2:4]:
        copy.wait()
    to, source = iota((CHUNKS * TILE, ROWS), 0), iota((CHUNKS * TILE, ROWS), 1)
    place = to % TILE
    row = to // TILE * CHUNK + place % CHUNK
    both = pick((source == row) & (place < CHUNK), k_ref[...])
    both = (both + pick((source == row) & (place >= CHUNK), v_ref[...])).astype(bf16)
    for z in range(RUNS * CHUNKS):
        i, j = z // CHUNKS, z % CHUNKS
        for h in range(HEADS_HERE):
            cols = slice(h * HEAD_DIM, (h + 1) * HEAD_DIM)
            out_ref[z * HEADS_HERE + h, 0:TILE, :] = queries[i * TILE : (i + 1) * TILE, cols]
            out_ref[z * HEADS_HERE + h, TILE : 2 * TILE, :] = both[j * TILE : (j + 1) * TILE, cols]

    for copy in copies[4:]:
        copy.wait()
    height, rows = LOCS * 2 * PAD, ROWS * PATCH
    to, source = iota((height, rows), 0), iota((height, rows), 1)
    place = to % TILE
    patch = to // TILE % RUNS * RUN + place
    moved = pick((source == patch * PATCH + to // PAD) & (place < RUN), e_ref[...])
    high, middle, low = three_parts(gain_ref[...])
    row = iota((height, COLS), 0) % (2 * PAD)
    moved = jnp.where(row == RUN, high, moved)
    moved = jnp.where(row == TILE + RUN, middle, moved)
    moved = jnp.where(row == PAD + RUN, low, moved)
    e_out[...] = moved.astype(bf16).reshape(LOCS, 2 * PAD, COLS)


def split(in_ref, out_ref):
    both = in_ref[:, TILE : 2 * TILE, :].astype(f32)
    out_ref[0:KN, :] = both[:, 0:CHUNK, :].reshape(KN, HEAD_DIM).astype(bf16)
    out_ref[KN : 2 * KN, :] = both[:, CHUNK:TILE, :].reshape(KN, HEAD_DIM).astype(bf16)
    numbers = in_ref[:, 0:TILE, :].astype(f32)[:, RUN:TILE, :]
    out_ref[2 * KN : 2 * KN + PEERS, :] = numbers.reshape(PEERS, HEAD_DIM).astype(bf16)


def run_starts(numbers):
    other = pltpu.roll(numbers, HEAD_DIM // 2, 1)
    lower = iota(numbers.shape, 1) < HEAD_DIM // 2
    return jnp.where(lower, numbers, other) * RUN, jnp.where(lower, other, numbers) * RUN


def key_positions(numbers, chunk):
    first, second = run_starts(numbers)
    dims = (PEERS, CHUNK, HEAD_DIM)
    row = iota(dims, 1) + chunk * CHUNK
    place = row.astype(f32)
    pos = jnp.where(
        row < RUN,
        jnp.broadcast_to(first[:, None, :], dims) + place,
        jnp.broadcast_to(second[:, None, :], dims) + (place - RUN),
    )
    return jnp.where(row < ROWS, pos, f32(FAR)).reshape(KN, HEAD_DIM)


def query_positions(numbers, run):
    first, second = run_starts(numbers)
    start = jnp.where(run == 0, first, second)
    dims = (PEERS, TILE, HEAD_DIM)
    row = iota(dims, 1)
    pos = jnp.broadcast_to(start[:, None, :], dims) + row.astype(f32)
    return jnp.where(row < RUN, pos, f32(-1)).reshape(QN, HEAD_DIM)


def attend(in_ref, kv_ref, out_ref, s_ref):
    scale = math.log2(math.e) / math.sqrt(HEAD_DIM)
    run = lax.axis_index("za")
    chunk = lax.axis_index("zb") * 2 + lax.axis_index("zc")
    queries = in_ref[:, 0:TILE, :]
    numbers = queries.astype(f32)[:, RUN:TILE, :].reshape(PEERS, HEAD_DIM)
    queries = queries.reshape(QN, HEAD_DIM)
    query_pos = query_positions(numbers, run).T[0:1, :]
    best = jnp.full((8, QN), FLOOR, f32)
    for core in range(2):
        key_pos = key_positions(kv_ref[core, 2 * KN : 2 * KN + PEERS, :].astype(f32), chunk)
        for n in range(KN // STEP):
            rows = slice(n * STEP, (n + 1) * STEP)
            scores = lax.dot_general(
                kv_ref[core, rows, :], queries, (((1,), (1,)), ((), ())), preferred_element_type=f32
            )
            spread = jnp.concatenate([key_pos[rows, :]] * (QN // HEAD_DIM), axis=1)
            scores = jnp.where(spread <= query_pos, scores * scale, f32(MASKED))
            s_ref[core * KN + n * STEP : core * KN + (n + 1) * STEP, :] = scores
            best = jnp.maximum(best, jnp.max(scores.reshape(STEP // 8, 8, QN), axis=0))
    best = jnp.max(best, axis=0, keepdims=True)
    total = jnp.zeros((8, QN), f32)
    acc = jnp.zeros((HEAD_DIM, QN), f32)
    for core in range(2):
        for n in range(KN // STEP):
            weights = jnp.exp2(s_ref[core * KN + n * STEP : core * KN + (n + 1) * STEP, :] - best)
            total = total + jnp.sum(weights.reshape(STEP // 8, 8, QN), axis=0)
            acc = acc + lax.dot_general(
                kv_ref[core, KN + n * STEP : KN + (n + 1) * STEP, :],
                weights.astype(bf16),
                (((0,), (0,)), ((), ())),
                preferred_element_type=f32,
            )
    total = jnp.sum(total, axis=0, keepdims=True)
    total = jnp.maximum(total, f32(1e-30))
    result = (acc * (1.0 / total)).T
    level = best + jnp.log(total) * math.log2(math.e)
    tiles = QN // 128
    level = jnp.concatenate([level[:, t * 128 : (t + 1) * 128] for t in range(tiles)], axis=0)
    parts = three_parts(level)
    lane = iota((tiles, 128), 1)
    row = iota((TILE, HEAD_DIM), 0)
    for slot in range(128 // TILE):
        shifts = [TILE * (n - slot) % 128 for n in range(3)]
        rolled = [pltpu.roll(x, s, 1) if s else x for x, s in zip(parts, shifts)]
        packed = jnp.where(lane < TILE, rolled[0], jnp.where(lane < 2 * TILE, rolled[1], rolled[2]))
        packed = jnp.where(lane < 3 * TILE, packed, f32(0))
        for t in range(tiles):
            block = t * (128 // TILE) + slot
            mine = result[block * TILE : (block + 1) * TILE, :]
            out_ref[block, :, :] = jnp.where(row < RUN, mine, packed[t : t + 1, :]).astype(bf16)


def finish(part_ref, w_ref, e_ref, out_ref):
    levels = part_ref[...].astype(f32)[:, RUN:TILE, :].reshape(PEERS, HEAD_DIM)
    levels = levels + pltpu.roll(levels, 128 - TILE, 1) + pltpu.roll(levels, 128 - 2 * TILE, 1)
    levels = levels.reshape(RUNS, CHUNKS, HEADS_HERE, 128)
    levels = jnp.exp2(levels - jnp.max(levels, axis=1, keepdims=True))
    shares = levels / jnp.sum(levels, axis=1, keepdims=True)
    shares = jnp.concatenate(
        [shares.reshape(PEERS, 128), jnp.zeros((128 - PEERS, 128), f32)], axis=0
    ).T
    real = iota((TILE, HEAD_DIM), 0) < RUN
    per_slot = SLOT_D // HEAD_DIM
    rows = []
    for u in range(2):
        for i in range(RUNS):
            heads = []
            for h in range(u * per_slot, (u + 1) * per_slot):
                acc = jnp.zeros((TILE, HEAD_DIM), f32)
                for j in range(CHUNKS):
                    block = (i * CHUNKS + j) * HEADS_HERE + h
                    acc = acc + shares[0:TILE, block : block + 1] * part_ref[block, :, :].astype(f32)
                heads.append(jnp.where(real, acc, f32(0)).astype(bf16))
            rows.append(jnp.concatenate(heads, axis=1))
    slots = jnp.concatenate(rows, axis=0)
    embed = jnp.concatenate([e_ref[part, :, :] for part in range(LOCS)], axis=1).astype(f32)
    gain = embed[RUN : RUN + 1, :] + embed[TILE + RUN : TILE + RUN + 1, :] + embed[PAD + RUN : PAD + RUN + 1, :]
    mixed = jnp.dot(slots, w_ref[...], preferred_element_type=f32) + embed
    spread = jnp.sum(mixed * mixed, axis=1, keepdims=True) / LOCAL_D + 1e-05
    normed = (mixed / jnp.sqrt(spread) * gain).astype(bf16)
    for part in range(LOCS):
        out_ref[part, :, :] = normed[:, part * COLS : (part + 1) * COLS]


def unpack(in_ref, out_ref):
    height, rows = LOCS * 2 * PAD, ROWS * PATCH
    to, source = iota((rows, height), 0), iota((rows, height), 1)
    patch = to // PATCH
    row = to % PATCH * PAD + patch // RUN * TILE + patch % RUN
    moved = pick(source == row, in_ref[...].reshape(height, COLS))
    out_ref[...] = moved.astype(bf16)


def vmem(count):
    return [pl.BlockSpec(memory_space=pltpu.VMEM)] * count


def call(kernel, outs, specs, scratch=(), flops=0, moved=0):
    return pl.pallas_call(
        kernel,
        out_shape=outs,
        in_specs=specs,
        out_specs=jax.tree.map(lambda _: pl.BlockSpec(memory_space=pltpu.VMEM), outs),
        scratch_shapes=scratch,
        compiler_params=pltpu.CompilerParams(vmem_limit_bytes=40 * 1024 * 1024),
        cost_estimate=pl.CostEstimate(flops=flops, bytes_accessed=moved, transcendentals=0),
        name=kernel.__name__,
    )


def shape(*dims):
    return jax.ShapeDtypeStruct(dims, bf16)


def on_device(queries, keys, values, positions, byte_embed, w_slot, gain):
    wide = (ROWS, HEADS_HERE * HEAD_DIM)
    sent, embed = call(
        pack,
        [shape(PEERS, 2 * TILE, HEAD_DIM), shape(LOCS, 2 * PAD, COLS)],
        [pl.BlockSpec(memory_space=pl.ANY)] * 6,
        [
            pltpu.SMEM((ROWS,), jnp.int32),
            pltpu.VMEM(wide, bf16),
            pltpu.VMEM(wide, bf16),
            pltpu.VMEM(wide, bf16),
            pltpu.VMEM((ROWS * PATCH, COLS), bf16),
            pltpu.VMEM((1, COLS), f32),
            pltpu.SemaphoreType.DMA((6,)),
        ],
    )(positions, queries, keys, values, byte_embed, gain.reshape(1, COLS))
    held = lax.all_to_all(sent, GROUP, split_axis=0, concat_axis=0, tiled=True)
    embed = lax.all_to_all(embed, "loc", split_axis=0, concat_axis=0, tiled=True)
    kv = call(split, shape(2 * KN + PEERS, HEAD_DIM), vmem(1))(held)
    kv = lax.all_gather(kv, "c", axis=0, tiled=False)
    partial = call(
        attend,
        shape(PEERS, TILE, HEAD_DIM),
        vmem(2),
        [pltpu.VMEM((2 * KN, QN), f32)],
        flops=4 * QN * 2 * KN * HEAD_DIM,
        moved=2 * 4 * KN * HEAD_DIM,
    )(held, kv)
    partial, embed = lax.optimization_barrier((partial, embed))
    partial = lax.all_to_all(partial, GROUP, split_axis=0, concat_axis=0, tiled=True)
    normed = call(finish, shape(LOCS, 2 * PAD, COLS), vmem(3))(partial, w_slot, embed)
    columns = lax.all_to_all(normed, "loc", split_axis=0, concat_axis=0, tiled=True)
    return call(unpack, shape(ROWS * PATCH, COLS), vmem(1))(columns)


def solution(mesh):
    devices = mesh.devices.reshape(2, 2, 2, 4, 2, 2, LOCS)
    finer = Mesh(devices, SEQ + ("loc",))
    placed = (
        P(SEQ, "loc"),
        P(SEQ, "loc"),
        P(SEQ, "loc"),
        P(SEQ),
        P(SEQ, "loc"),
        P(),
        P("loc"),
    )
    return jax.shard_map(
        on_device, mesh=finer, in_specs=placed, out_specs=P(SEQ, "loc"), check_vma=False
    )
```

```python
import math

import jax
import jax.numpy as jnp
from jax import lax
from jax.experimental import pallas as pl
from jax.experimental.pallas import tpu as pltpu
from jax.sharding import Mesh
from jax.sharding import PartitionSpec as P

HEAD_DIM = 128
PATCH = 8
RUN = 15
RUNS = 2
ROWS = RUN * RUNS
TILE = 16
PAD = RUNS * TILE
CHUNK = 8
CHUNKS = 4
HEADS_HERE = 8
LOCAL_D = 1024
SLOT_D = 512
LOCS = 4
COLS = LOCAL_D // LOCS
SEQ = ("za", "zb", "zc", "x", "yl", "c")
GROUP = ("za", "zb", "zc", "x", "yl")
PEERS = RUNS * CHUNKS * HEADS_HERE
QN = PEERS * TILE
KN = PEERS * CHUNK
STEP = 256
FLOOR = -1e20
MASKED = -1e30
FAR = 1e6
bf16 = jnp.bfloat16
f32 = jnp.float32


def iota(shape, dim):
    return lax.broadcasted_iota(jnp.int32, shape, dim)


def pick(condition, rows):
    select = jnp.where(condition, f32(1), f32(0)).astype(bf16)
    return jnp.dot(select, rows, preferred_element_type=f32)


def three_parts(x):
    high = x.astype(bf16).astype(f32)
    middle = (x - high).astype(bf16).astype(f32)
    return high, middle, x - high - middle


def pack(
    pos_hbm,
    q_hbm,
    k_hbm,
    v_hbm,
    e_hbm,
    gain_hbm,
    out_ref,
    own_out,
    next_out,
    across_out,
    last_out,
    pos_ref,
    q_ref,
    k_ref,
    v_ref,
    e_ref,
    gain_ref,
    sems,
):
    pairs = [
        (pos_hbm, pos_ref),
        (q_hbm, q_ref),
        (k_hbm, k_ref),
        (v_hbm, v_ref),
        (e_hbm, e_ref),
        (gain_hbm, gain_ref),
    ]
    copies = [pltpu.make_async_copy(a, b, sems.at[n]) for n, (a, b) in enumerate(pairs)]
    for copy in copies:
        copy.start()
    for copy in copies[:2]:
        copy.wait()

    wide = (PAD, HEADS_HERE * HEAD_DIM)
    to, source = iota((PAD, ROWS), 0), iota((PAD, ROWS), 1)
    place = to % TILE
    queries = pick((source == to // TILE * RUN + place) & (place < RUN), q_ref[...])
    first = (pos_ref[0] // RUN).astype(f32)
    second = (pos_ref[RUN] // RUN).astype(f32)
    numbers = jnp.where(iota(wide, 1) % HEAD_DIM < HEAD_DIM // 2, first, second)
    queries = jnp.where(iota(wide, 0) % TILE == RUN, numbers, queries).astype(bf16)

    for copy in copies[2:4]:
        copy.wait()
    to, source = iota((CHUNKS * TILE, ROWS), 0), iota((CHUNKS * TILE, ROWS), 1)
    place = to % TILE
    row = to // TILE * CHUNK + place % CHUNK
    both = pick((source == row) & (place < CHUNK), k_ref[...])
    both = (both + pick((source == row) & (place >= CHUNK), v_ref[...])).astype(bf16)
    for z in range(RUNS * CHUNKS):
        i, j = z // CHUNKS, z % CHUNKS
        for h in range(HEADS_HERE):
            cols = slice(h * HEAD_DIM, (h + 1) * HEAD_DIM)
            out_ref[z * HEADS_HERE + h, 0:TILE, :] = queries[i * TILE : (i + 1) * TILE, cols]
            out_ref[z * HEADS_HERE + h, TILE : 2 * TILE, :] = both[j * TILE : (j + 1) * TILE, cols]

    for copy in copies[4:]:
        copy.wait()
    height, rows = LOCS * 2 * PAD, ROWS * PATCH
    to, source = iota((height, rows), 0), iota((height, rows), 1)
    place = to % TILE
    patch = to // TILE % RUNS * RUN + place
    target = (to // (2 * PAD) + lax.axis_index("loc")) % LOCS
    slot = target * 2 + to // PAD % 2
    moved = pick((source == patch * PATCH + slot) & (place < RUN), e_ref[...])
    high, middle, low = three_parts(gain_ref[...])
    row = iota((height, COLS), 0) % (2 * PAD)
    moved = jnp.where(row == RUN, high, moved)
    moved = jnp.where(row == TILE + RUN, middle, moved)
    moved = jnp.where(row == PAD + RUN, low, moved)
    moved = moved.astype(bf16)
    for step, ref in enumerate((own_out, next_out, across_out, last_out)):
        ref[...] = moved[step * 2 * PAD : (step + 1) * 2 * PAD, :]


def split(in_ref, out_ref):
    both = in_ref[:, TILE : 2 * TILE, :].astype(f32)
    out_ref[0:KN, :] = both[:, 0:CHUNK, :].reshape(KN, HEAD_DIM).astype(bf16)
    out_ref[KN : 2 * KN, :] = both[:, CHUNK:TILE, :].reshape(KN, HEAD_DIM).astype(bf16)
    numbers = in_ref[:, 0:TILE, :].astype(f32)[:, RUN:TILE, :]
    out_ref[2 * KN : 2 * KN + PEERS, :] = numbers.reshape(PEERS, HEAD_DIM).astype(bf16)


def run_starts(numbers):
    other = pltpu.roll(numbers, HEAD_DIM // 2, 1)
    lower = iota(numbers.shape, 1) < HEAD_DIM // 2
    return jnp.where(lower, numbers, other) * RUN, jnp.where(lower, other, numbers) * RUN


def key_positions(numbers, chunk):
    first, second = run_starts(numbers)
    dims = (PEERS, CHUNK, HEAD_DIM)
    row = iota(dims, 1) + chunk * CHUNK
    place = row.astype(f32)
    pos = jnp.where(
        row < RUN,
        jnp.broadcast_to(first[:, None, :], dims) + place,
        jnp.broadcast_to(second[:, None, :], dims) + (place - RUN),
    )
    return jnp.where(row < ROWS, pos, f32(FAR)).reshape(KN, HEAD_DIM)


def query_positions(numbers, run):
    first, second = run_starts(numbers)
    start = jnp.where(run == 0, first, second)
    dims = (PEERS, TILE, HEAD_DIM)
    row = iota(dims, 1)
    pos = jnp.broadcast_to(start[:, None, :], dims) + row.astype(f32)
    return jnp.where(row < RUN, pos, f32(-1)).reshape(QN, HEAD_DIM)


def attend(in_ref, kv_ref, out_ref, s_ref):
    scale = math.log2(math.e) / math.sqrt(HEAD_DIM)
    run = lax.axis_index("za")
    chunk = lax.axis_index("zb") * 2 + lax.axis_index("zc")
    queries = in_ref[:, 0:TILE, :]
    numbers = queries.astype(f32)[:, RUN:TILE, :].reshape(PEERS, HEAD_DIM)
    queries = queries.reshape(QN, HEAD_DIM)
    query_pos = query_positions(numbers, run).T[0:1, :]
    best = jnp.full((8, QN), FLOOR, f32)
    for core in range(2):
        key_pos = key_positions(kv_ref[core, 2 * KN : 2 * KN + PEERS, :].astype(f32), chunk)
        for n in range(KN // STEP):
            rows = slice(n * STEP, (n + 1) * STEP)
            scores = lax.dot_general(
                kv_ref[core, rows, :], queries, (((1,), (1,)), ((), ())), preferred_element_type=f32
            )
            spread = jnp.concatenate([key_pos[rows, :]] * (QN // HEAD_DIM), axis=1)
            scores = jnp.where(spread <= query_pos, scores * scale, f32(MASKED))
            s_ref[core * KN + n * STEP : core * KN + (n + 1) * STEP, :] = scores
            best = jnp.maximum(best, jnp.max(scores.reshape(STEP // 8, 8, QN), axis=0))
    best = jnp.max(best, axis=0, keepdims=True)
    total = jnp.zeros((8, QN), f32)
    acc = jnp.zeros((HEAD_DIM, QN), f32)
    for core in range(2):
        for n in range(KN // STEP):
            weights = jnp.exp2(s_ref[core * KN + n * STEP : core * KN + (n + 1) * STEP, :] - best)
            total = total + jnp.sum(weights.reshape(STEP // 8, 8, QN), axis=0)
            acc = acc + lax.dot_general(
                kv_ref[core, KN + n * STEP : KN + (n + 1) * STEP, :],
                weights.astype(bf16),
                (((0,), (0,)), ((), ())),
                preferred_element_type=f32,
            )
    total = jnp.sum(total, axis=0, keepdims=True)
    total = jnp.maximum(total, f32(1e-30))
    result = (acc * (1.0 / total)).T
    level = best + jnp.log(total) * math.log2(math.e)
    tiles = QN // 128
    level = jnp.concatenate([level[:, t * 128 : (t + 1) * 128] for t in range(tiles)], axis=0)
    parts = three_parts(level)
    lane = iota((tiles, 128), 1)
    row = iota((TILE, HEAD_DIM), 0)
    for slot in range(128 // TILE):
        shifts = [TILE * (n - slot) % 128 for n in range(3)]
        rolled = [pltpu.roll(x, s, 1) if s else x for x, s in zip(parts, shifts)]
        packed = jnp.where(lane < TILE, rolled[0], jnp.where(lane < 2 * TILE, rolled[1], rolled[2]))
        packed = jnp.where(lane < 3 * TILE, packed, f32(0))
        for t in range(tiles):
            block = t * (128 // TILE) + slot
            mine = result[block * TILE : (block + 1) * TILE, :]
            out_ref[block, :, :] = jnp.where(row < RUN, mine, packed[t : t + 1, :]).astype(bf16)


def finish(part_ref, w_ref, own_ref, next_ref, across_ref, last_ref, out_ref, e_ref):
    for step, ref in enumerate((own_ref, next_ref, across_ref, last_ref)):
        origin = (lax.axis_index("loc") + LOCS - step) % LOCS
        e_ref[:, pl.ds(pl.multiple_of(origin * COLS, COLS), COLS)] = ref[...]
    levels = part_ref[...].astype(f32)[:, RUN:TILE, :].reshape(PEERS, HEAD_DIM)
    levels = levels + pltpu.roll(levels, 128 - TILE, 1) + pltpu.roll(levels, 128 - 2 * TILE, 1)
    levels = levels.reshape(RUNS, CHUNKS, HEADS_HERE, 128)
    levels = jnp.exp2(levels - jnp.max(levels, axis=1, keepdims=True))
    shares = levels / jnp.sum(levels, axis=1, keepdims=True)
    shares = jnp.concatenate(
        [shares.reshape(PEERS, 128), jnp.zeros((128 - PEERS, 128), f32)], axis=0
    ).T
    real = iota((TILE, HEAD_DIM), 0) < RUN
    per_slot = SLOT_D // HEAD_DIM
    rows = []
    for u in range(2):
        for i in range(RUNS):
            heads = []
            for h in range(u * per_slot, (u + 1) * per_slot):
                acc = jnp.zeros((TILE, HEAD_DIM), f32)
                for j in range(CHUNKS):
                    block = (i * CHUNKS + j) * HEADS_HERE + h
                    acc = acc + shares[0:TILE, block : block + 1] * part_ref[block, :, :].astype(f32)
                heads.append(jnp.where(real, acc, f32(0)).astype(bf16))
            rows.append(jnp.concatenate(heads, axis=1))
    slots = jnp.concatenate(rows, axis=0)
    embed = e_ref[...].astype(f32)
    gain = embed[RUN : RUN + 1, :] + embed[TILE + RUN : TILE + RUN + 1, :] + embed[PAD + RUN : PAD + RUN + 1, :]
    mixed = jnp.dot(slots, w_ref[...], preferred_element_type=f32) + embed
    spread = jnp.sum(mixed * mixed, axis=1, keepdims=True) / LOCAL_D + 1e-05
    normed = (mixed / jnp.sqrt(spread) * gain).astype(bf16)
    for part in range(LOCS):
        out_ref[part, :, :] = normed[:, part * COLS : (part + 1) * COLS]


def unpack(in_ref, out_ref):
    height, rows = LOCS * 2 * PAD, ROWS * PATCH
    to, source = iota((rows, height), 0), iota((rows, height), 1)
    patch = to // PATCH
    row = to % PATCH * PAD + patch // RUN * TILE + patch % RUN
    moved = pick(source == row, in_ref[...].reshape(height, COLS))
    out_ref[...] = moved.astype(bf16)


def vmem(count):
    return [pl.BlockSpec(memory_space=pltpu.VMEM)] * count


def call(kernel, outs, specs, scratch=(), flops=0, moved=0, limit=40 * 1024 * 1024):
    return pl.pallas_call(
        kernel,
        out_shape=outs,
        in_specs=specs,
        out_specs=jax.tree.map(lambda _: pl.BlockSpec(memory_space=pltpu.VMEM), outs),
        scratch_shapes=scratch,
        compiler_params=pltpu.CompilerParams(vmem_limit_bytes=limit),
        cost_estimate=pl.CostEstimate(flops=flops, bytes_accessed=moved, transcendentals=0),
        name=kernel.__name__,
    )


def shape(*dims):
    return jax.ShapeDtypeStruct(dims, bf16)


def along(block, steps):
    return lax.ppermute(block, "loc", [(i, (i + steps) % LOCS) for i in range(LOCS)])


def on_device(queries, keys, values, positions, byte_embed, w_slot, gain):
    wide = (ROWS, HEADS_HERE * HEAD_DIM)
    sent, *embed = call(
        pack,
        [shape(PEERS, 2 * TILE, HEAD_DIM)] + [shape(2 * PAD, COLS)] * LOCS,
        [pl.BlockSpec(memory_space=pltpu.HBM)] * 6,
        [
            pltpu.SMEM((ROWS,), jnp.int32),
            pltpu.VMEM(wide, bf16),
            pltpu.VMEM(wide, bf16),
            pltpu.VMEM(wide, bf16),
            pltpu.VMEM((ROWS * PATCH, COLS), bf16),
            pltpu.VMEM((1, COLS), f32),
            pltpu.SemaphoreType.DMA((6,)),
        ],
        limit=None,
    )(positions, queries, keys, values, byte_embed, gain.reshape(1, COLS))
    held = lax.all_to_all(sent, GROUP, split_axis=0, concat_axis=0, tiled=True)
    held, step_one, step_two = lax.optimization_barrier(
        (held, along(embed[1], 1), along(embed[2], 2))
    )
    kv = call(split, shape(2 * KN + PEERS, HEAD_DIM), vmem(1))(held)
    kv = lax.all_gather(kv, "c", axis=0, tiled=False)
    partial = call(
        attend,
        shape(PEERS, TILE, HEAD_DIM),
        vmem(2),
        [pltpu.VMEM((2 * KN, QN), f32)],
        flops=4 * QN * 2 * KN * HEAD_DIM,
        moved=2 * 4 * KN * HEAD_DIM,
    )(held, kv)
    partial, last = lax.optimization_barrier((partial, embed[3]))
    embed = [embed[0], step_one, step_two, along(last, 3)]
    partial = lax.all_to_all(partial, GROUP, split_axis=0, concat_axis=0, tiled=True)
    normed = call(
        finish,
        shape(LOCS, 2 * PAD, COLS),
        vmem(2 + LOCS),
        [pltpu.VMEM((2 * PAD, LOCAL_D), bf16)],
    )(partial, w_slot, *embed)
    columns = lax.all_to_all(normed, "loc", split_axis=0, concat_axis=0, tiled=True)
    return call(unpack, shape(ROWS * PATCH, COLS), vmem(1))(columns)


def solution(mesh):
    devices = mesh.devices.reshape(2, 2, 2, 4, 2, 2, LOCS)
    finer = Mesh(devices, SEQ + ("loc",))
    placed = (
        P(SEQ, "loc"),
        P(SEQ, "loc"),
        P(SEQ, "loc"),
        P(SEQ),
        P(SEQ, "loc"),
        P(),
        P("loc"),
    )
    return jax.shard_map(
        on_device, mesh=finer, in_specs=placed, out_specs=P(SEQ, "loc"), check_vma=False
    )
```

```python
import math

import jax
import jax.numpy as jnp
from jax import lax
from jax.experimental import pallas as pl
from jax.experimental.pallas import tpu as pltpu
from jax.sharding import Mesh
from jax.sharding import PartitionSpec as P

HEAD_DIM = 128
PATCH = 8
RUN = 15
RUNS = 2
ROWS = RUN * RUNS
TILE = 16
PAD = RUNS * TILE
CHUNK = 8
CHUNKS = 4
HEADS_HERE = 8
LOCAL_D = 1024
SLOT_D = 512
LOCS = 4
COLS = LOCAL_D // LOCS
SEQ = ("za", "zb", "zc", "x", "yl", "c")
EVERY = SEQ + ("loc",)
DEPTH, PLANE = 8, 8
DEPTH_ORDER = (7, 5, 3, 1, 6, 4, 2, 0)
HOME_ORDER = (7, 5, 3, 1, 6, 4, 2, 0)
HOME_PLACE = tuple(HOME_ORDER.index(z) for z in DEPTH_ORDER)
LOC_ORDER = (2, 3, 1, 0)
SHARDS = DEPTH * PLANE * 2
PEERS = RUNS * CHUNKS * HEADS_HERE
QN = PEERS * TILE
KN = PEERS * CHUNK
STEP = 256
FLOOR = -1e20
MASKED = -1e30
FAR = 1e6
bf16 = jnp.bfloat16
f32 = jnp.float32


def iota(shape, dim):
    return lax.broadcasted_iota(jnp.int32, shape, dim)


def pick(condition, rows):
    select = jnp.where(condition, f32(1), f32(0)).astype(bf16)
    return jnp.dot(select, rows, preferred_element_type=f32)


def three_parts(x):
    high = x.astype(bf16).astype(f32)
    middle = (x - high).astype(bf16).astype(f32)
    return high, middle, x - high - middle


def exchange(blocks, groups):
    return lax.all_to_all(
        blocks, EVERY, split_axis=0, concat_axis=0, tiled=True, axis_index_groups=groups
    )


def seq_groups(depth_order):
    return [
        [((z * PLANE + spot) * 2 + core) * LOCS + loc for z in depth_order for spot in range(PLANE)]
        for core in range(2)
        for loc in range(LOCS)
    ]


def loc_groups():
    return [[shard * LOCS + loc for loc in LOC_ORDER] for shard in range(SHARDS)]


def start_all(pairs, sems):
    copies = [pltpu.make_async_copy(a, b, sems.at[n]) for n, (a, b) in enumerate(pairs)]
    for copy in copies:
        copy.start()
    return copies


def pack(pos_hbm, q_hbm, k_hbm, v_hbm, out_hbm, pos_ref, q_ref, k_ref, v_ref, out_ref, sems, out_sems):
    copies = start_all([(pos_hbm, pos_ref), (q_hbm, q_ref), (k_hbm, k_ref), (v_hbm, v_ref)], sems)
    for copy in copies[:2]:
        copy.wait()

    wide = (PAD, HEADS_HERE * HEAD_DIM)
    to, source = iota((PAD, ROWS), 0), iota((PAD, ROWS), 1)
    place = to % TILE
    queries = pick((source == to // TILE * RUN + place) & (place < RUN), q_ref[...])
    first = (pos_ref[0] // RUN).astype(f32)
    second = (pos_ref[RUN] // RUN).astype(f32)
    numbers = jnp.where(iota(wide, 1) % HEAD_DIM < HEAD_DIM // 2, first, second)
    queries = jnp.where(iota(wide, 0) % TILE == RUN, numbers, queries).astype(bf16)

    for copy in copies[2:]:
        copy.wait()
    to, source = iota((CHUNKS * TILE, ROWS), 0), iota((CHUNKS * TILE, ROWS), 1)
    place = to % TILE
    row = to // TILE * CHUNK + place % CHUNK
    both = pick((source == row) & (place < CHUNK), k_ref[...])
    both = (both + pick((source == row) & (place >= CHUNK), v_ref[...])).astype(bf16)
    sent = []
    for z in range(RUNS * CHUNKS):
        i, j = z // CHUNKS, z % CHUNKS
        for h in range(HEADS_HERE):
            cols = slice(h * HEAD_DIM, (h + 1) * HEAD_DIM)
            out_ref[z * HEADS_HERE + h, 0:TILE, :] = queries[i * TILE : (i + 1) * TILE, cols]
            out_ref[z * HEADS_HERE + h, TILE : 2 * TILE, :] = both[j * TILE : (j + 1) * TILE, cols]
        mine = pl.ds(z * HEADS_HERE, HEADS_HERE)
        sent.append(pltpu.make_async_copy(out_ref.at[mine], out_hbm.at[mine], out_sems.at[z]))
        sent[-1].start()
    for copy in sent:
        copy.wait()


def pack_embed(e_ref, gain_ref, own_out, first_out, second_out):
    height, rows = LOCS * 2 * PAD, ROWS * PATCH
    to, source = iota((height, rows), 0), iota((height, rows), 1)
    place = to % TILE
    patch = to // TILE % RUNS * RUN + place
    slot = (to // (2 * PAD) ^ lax.axis_index("loc")) * 2 + to // PAD % 2
    moved = pick((source == patch * PATCH + slot) & (place < RUN), e_ref[...])
    high, middle, low = three_parts(gain_ref[...])
    row = iota((height, COLS), 0) % (2 * PAD)
    moved = jnp.where(row == RUN, high, moved)
    moved = jnp.where(row == TILE + RUN, middle, moved)
    moved = jnp.where(row == PAD + RUN, low, moved).astype(bf16)
    step = [moved[n * 2 * PAD : (n + 1) * 2 * PAD, :] for n in range(LOCS)]
    own_out[...] = step[0]
    first_out[0, :, :] = step[1]
    first_out[1, :, :] = step[3]
    second_out[...] = step[2]


def split(in_ref, out_ref):
    both = in_ref[:, TILE : 2 * TILE, :].astype(f32)
    out_ref[0:KN, :] = both[:, 0:CHUNK, :].reshape(KN, HEAD_DIM).astype(bf16)
    out_ref[KN : 2 * KN, :] = both[:, CHUNK:TILE, :].reshape(KN, HEAD_DIM).astype(bf16)
    numbers = in_ref[:, 0:TILE, :].astype(f32)[:, RUN:TILE, :]
    out_ref[2 * KN : 2 * KN + PEERS, :] = numbers.reshape(PEERS, HEAD_DIM).astype(bf16)


def run_starts(numbers):
    other = pltpu.roll(numbers, HEAD_DIM // 2, 1)
    lower = iota(numbers.shape, 1) < HEAD_DIM // 2
    return jnp.where(lower, numbers, other) * RUN, jnp.where(lower, other, numbers) * RUN


def key_positions(numbers, chunk):
    spot = iota((PEERS, KN), 1) // CHUNK == iota((PEERS, KN), 0)
    spot = jnp.where(spot, f32(1), f32(0)).astype(bf16)
    both = lax.dot_general(
        numbers, spot, (((0,), (0,)), ((), ())), preferred_element_type=f32
    )
    half = HEAD_DIM // 2
    first, second = both[0:8, :] * RUN, both[half : half + 8, :] * RUN
    row = iota((8, KN), 1) % CHUNK + chunk * CHUNK
    place = row.astype(f32)
    pos = jnp.where(row < RUN, first + place, second + (place - RUN))
    return jnp.where(row < ROWS, pos, f32(FAR))[0:1, :]


def attend(in_ref, kv_ref, out_hbm, out_ref, s_ref, sems):
    scale = math.log2(math.e) / math.sqrt(HEAD_DIM)
    run = 1 - lax.axis_index("zc")
    chunk = 3 - (lax.axis_index("za") * 2 + lax.axis_index("zb"))
    key_pos, values = [], []
    for core in range(2):
        key_pos.append(key_positions(kv_ref[core, 2 * KN : 2 * KN + PEERS, :], chunk))
        ones = jnp.ones((KN, HEAD_DIM), bf16)
        values.append(jnp.concatenate([kv_ref[core, KN : 2 * KN, :], ones], axis=1))
    numbers = in_ref[:, 0:TILE, :].astype(f32)[:, RUN:TILE, :].reshape(PEERS, HEAD_DIM)
    first, second = run_starts(numbers)
    start = jnp.where(run == 0, first, second)
    blocks = STEP // TILE
    line = iota((blocks, TILE, HEAD_DIM), 1)
    lane = iota((blocks, TILE, HEAD_DIM), 2)
    own = (lane % TILE == line) & (lane < 3 * TILE)
    side = iota((blocks, HEAD_DIM), 1) // TILE
    copies = KN // HEAD_DIM
    sent = []
    for t in range(QN // STEP):
        tile = slice(t * blocks, (t + 1) * blocks)
        queries = in_ref[tile, 0:TILE, :].reshape(STEP, HEAD_DIM)
        pos = jnp.broadcast_to(start[tile, None, :], line.shape) + line.astype(f32)
        pos = jnp.where(line < RUN, pos, f32(-1)).reshape(STEP, HEAD_DIM)
        pos = jnp.concatenate([pos] * copies, axis=1)
        best = jnp.full((STEP, HEAD_DIM), FLOOR, f32)
        for core in range(2):
            scores = lax.dot_general(
                queries, kv_ref[core, 0:KN, :], (((1,), (1,)), ((), ())), preferred_element_type=f32
            )
            scores = jnp.where(key_pos[core] <= pos, scores * scale, f32(MASKED))
            s_ref[core, :, :] = scores
            for n in range(copies):
                best = jnp.maximum(best, scores[:, n * HEAD_DIM : (n + 1) * HEAD_DIM])
        best = jnp.broadcast_to(jnp.max(best, axis=1, keepdims=True), best.shape)
        wide = jnp.concatenate([best] * copies, axis=1)
        acc = jnp.zeros((STEP, 2 * HEAD_DIM), f32)
        for core in range(2):
            weights = jnp.exp2(s_ref[core, :, :] - wide).astype(bf16)
            acc = acc + jnp.dot(weights, values[core], preferred_element_type=f32)
        total = jnp.maximum(acc[:, HEAD_DIM:], f32(1e-30))
        result = (acc[:, 0:HEAD_DIM] / total).reshape(line.shape)
        best = jnp.sum(jnp.where(own, best.reshape(own.shape), f32(0)), axis=1)
        total = jnp.sum(jnp.where(own, total.reshape(own.shape), f32(0)), axis=1)
        level = best + jnp.log(jnp.maximum(total, f32(1e-30))) * math.log2(math.e)
        high, middle, low = three_parts(level)
        level = jnp.where(side == 0, high, jnp.where(side == 1, middle, low))
        level = jnp.where(side < 3, level, f32(0))
        level = jnp.broadcast_to(level[:, None, :], line.shape)
        out_ref[tile, :, :] = jnp.where(line < RUN, result, level).astype(bf16)
        for depth in range(t * blocks // PLANE, (t + 1) * blocks // PLANE):
            mine = out_ref.at[pl.ds(depth * PLANE, PLANE)]
            home = out_hbm.at[pl.ds(HOME_PLACE[depth] * PLANE, PLANE)]
            sent.append(pltpu.make_async_copy(mine, home, sems.at[depth]))
            sent[-1].start()
    for copy in sent:
        copy.wait()


def finish(part_ref, w_ref, own_ref, first_ref, second_ref, out_ref, e_ref):
    arrived = (own_ref[...], first_ref[0, :, :], second_ref[0, :, :], second_ref[1, :, :])
    for step, block in enumerate(arrived):
        origin = lax.axis_index("loc") ^ step
        e_ref[:, pl.ds(pl.multiple_of(origin * COLS, COLS), COLS)] = block
    levels = part_ref[...].astype(f32)[:, RUN:TILE, :].reshape(PEERS, HEAD_DIM)
    levels = levels + pltpu.roll(levels, 128 - TILE, 1) + pltpu.roll(levels, 128 - 2 * TILE, 1)
    levels = jnp.concatenate(
        [levels[at * PLANE : (at + 1) * PLANE, :] for at in HOME_PLACE], axis=0
    ).reshape(RUNS, CHUNKS, HEADS_HERE, 128)
    levels = jnp.exp2(levels - jnp.max(levels, axis=1, keepdims=True))
    shares = levels / jnp.sum(levels, axis=1, keepdims=True)
    shares = jnp.concatenate(
        [shares.reshape(PEERS, 128), jnp.zeros((128 - PEERS, 128), f32)], axis=0
    ).T
    real = iota((TILE, HEAD_DIM), 0) < RUN
    per_slot = SLOT_D // HEAD_DIM
    rows = []
    for u in range(2):
        for i in range(RUNS):
            heads = []
            for h in range(u * per_slot, (u + 1) * per_slot):
                acc = jnp.zeros((TILE, HEAD_DIM), f32)
                for j in range(CHUNKS):
                    block = (i * CHUNKS + j) * HEADS_HERE + h
                    partial = part_ref[HOME_PLACE[block // PLANE] * PLANE + h, :, :].astype(f32)
                    acc = acc + shares[0:TILE, block : block + 1] * partial
                heads.append(jnp.where(real, acc, f32(0)).astype(bf16))
            rows.append(jnp.concatenate(heads, axis=1))
    slots = jnp.concatenate(rows, axis=0)
    embed = e_ref[...].astype(f32)
    gain = embed[RUN : RUN + 1, :] + embed[TILE + RUN : TILE + RUN + 1, :] + embed[PAD + RUN : PAD + RUN + 1, :]
    mixed = jnp.dot(slots, w_ref[...], preferred_element_type=f32) + embed
    spread = jnp.sum(mixed * mixed, axis=1, keepdims=True) / LOCAL_D + 1e-05
    normed = (mixed / jnp.sqrt(spread) * gain).astype(bf16)
    for part in range(LOCS):
        out_ref[LOC_ORDER.index(part), :, :] = normed[:, part * COLS : (part + 1) * COLS]


def unpack(in_ref, out_ref):
    height, rows = LOCS * 2 * PAD, ROWS * PATCH
    to, source = iota((rows, height), 0), iota((rows, height), 1)
    patch = to // PATCH
    row = to % PATCH * PAD + patch // RUN * TILE + patch % RUN
    arrived = jnp.concatenate([in_ref[LOC_ORDER.index(loc), :, :] for loc in range(LOCS)], axis=0)
    moved = pick(source == row, arrived)
    out_ref[...] = moved.astype(bf16)


def vmem(count):
    return [pl.BlockSpec(memory_space=pltpu.VMEM)] * count


def call(kernel, outs, specs, scratch=(), flops=0, moved=0, limit=40 * 1024 * 1024, to_hbm=False):
    space = pltpu.HBM if to_hbm else pltpu.VMEM
    return pl.pallas_call(
        kernel,
        out_shape=outs,
        in_specs=specs,
        out_specs=jax.tree.map(lambda _: pl.BlockSpec(memory_space=space), outs),
        scratch_shapes=scratch,
        compiler_params=pltpu.CompilerParams(vmem_limit_bytes=limit),
        cost_estimate=pl.CostEstimate(flops=flops, bytes_accessed=moved, transcendentals=0),
        name=kernel.__name__,
    )


def shape(*dims):
    return jax.ShapeDtypeStruct(dims, bf16)


def swapped(block, step):
    return lax.ppermute(block, "loc", [(i, i ^ step) for i in range(LOCS)])


def on_device(queries, keys, values, positions, byte_embed, w_slot, gain):
    wide = (ROWS, HEADS_HERE * HEAD_DIM)
    messages = (PEERS, 2 * TILE, HEAD_DIM)
    results = (PEERS, TILE, HEAD_DIM)
    sent = call(
        pack,
        shape(*messages),
        [pl.BlockSpec(memory_space=pltpu.HBM)] * 4,
        [
            pltpu.SMEM((ROWS,), jnp.int32),
            pltpu.VMEM(wide, bf16),
            pltpu.VMEM(wide, bf16),
            pltpu.VMEM(wide, bf16),
            pltpu.VMEM(messages, bf16),
            pltpu.SemaphoreType.DMA((4,)),
            pltpu.SemaphoreType.DMA((RUNS * CHUNKS,)),
        ],
        limit=None,
        to_hbm=True,
    )(positions, queries, keys, values)
    sent, byte_embed = lax.optimization_barrier((sent, byte_embed))
    held = exchange(sent, seq_groups(DEPTH_ORDER))
    own, first, second = call(
        pack_embed,
        [shape(2 * PAD, COLS), shape(2, 2 * PAD, COLS), shape(2 * PAD, COLS)],
        vmem(2),
    )(byte_embed, gain.reshape(1, COLS))
    held, first = lax.optimization_barrier((held, swapped(first, 1)))
    kv = call(split, shape(2 * KN + PEERS, HEAD_DIM), vmem(1))(held)
    kv = lax.all_gather(kv, "c", axis=0, tiled=False)
    partial = call(
        attend,
        shape(*results),
        vmem(2),
        [
            pltpu.VMEM(results, bf16),
            pltpu.VMEM((2, STEP, KN), f32),
            pltpu.SemaphoreType.DMA((DEPTH,)),
        ],
        flops=4 * QN * 2 * KN * HEAD_DIM,
        moved=2 * 4 * KN * HEAD_DIM,
        to_hbm=True,
    )(held, kv)
    partial, first, second = lax.optimization_barrier((partial, first, second))
    second = swapped(jnp.stack([second, first[1]]), 2)
    partial = exchange(partial, seq_groups(HOME_ORDER))
    normed = call(
        finish,
        shape(LOCS, 2 * PAD, COLS),
        vmem(5),
        [pltpu.VMEM((2 * PAD, LOCAL_D), bf16)],
    )(partial, w_slot, own, first, second)
    columns = exchange(normed, loc_groups())
    return call(unpack, shape(ROWS * PATCH, COLS), vmem(1))(columns)


def solution(mesh):
    devices = mesh.devices.reshape(2, 2, 2, 4, 2, 2, LOCS)
    finer = Mesh(devices, SEQ + ("loc",))
    placed = (
        P(SEQ, "loc"),
        P(SEQ, "loc"),
        P(SEQ, "loc"),
        P(SEQ),
        P(SEQ, "loc"),
        P(),
        P("loc"),
    )
    return jax.shard_map(
        on_device, mesh=finer, in_specs=placed, out_specs=P(SEQ, "loc"), check_vma=False
    )
```

```python
import math

import jax
import jax.numpy as jnp
from jax import lax
from jax.experimental import pallas as pl
from jax.experimental.pallas import tpu as pltpu
from jax.sharding import Mesh
from jax.sharding import PartitionSpec as P

HEAD_DIM = 128
PATCH = 8
RUN = 15
RUNS = 2
ROWS = RUN * RUNS
TILE = 16
PAD = RUNS * TILE
CHUNK = 8
CHUNKS = 4
HEADS_HERE = 8
LOCAL_D = 1024
SLOT_D = 512
LOCS = 4
COLS = LOCAL_D // LOCS
SEQ = ("za", "zb", "zc", "x", "yl", "c")
EVERY = SEQ + ("loc",)
DEPTH, PLANE = 8, 8
DEPTH_ORDER = (7, 3, 1, 5, 6, 2, 0, 4)
HOME_ORDER = (7, 3, 1, 5, 6, 2, 0, 4)
HOME_PLACE = tuple(HOME_ORDER.index(z) for z in DEPTH_ORDER)
LOC_ORDER = (2, 3, 1, 0)
SHARDS = DEPTH * PLANE * 2
PEERS = RUNS * CHUNKS * HEADS_HERE
QN = PEERS * TILE
KN = PEERS * CHUNK
STEP = 256
FLOOR = -1e20
MASKED = -1e30
FAR = 1e6
bf16 = jnp.bfloat16
f32 = jnp.float32


def iota(shape, dim):
    return lax.broadcasted_iota(jnp.int32, shape, dim)


def pick(condition, rows):
    select = jnp.where(condition, f32(1), f32(0)).astype(bf16)
    return jnp.dot(select, rows, preferred_element_type=f32)


def three_parts(x):
    high = x.astype(bf16).astype(f32)
    middle = (x - high).astype(bf16).astype(f32)
    return high, middle, x - high - middle


def exchange(blocks, groups):
    return lax.all_to_all(
        blocks, EVERY, split_axis=0, concat_axis=0, tiled=True, axis_index_groups=groups
    )


def seq_groups(depth_order):
    return [
        [((z * PLANE + spot) * 2 + core) * LOCS + loc for z in depth_order for spot in range(PLANE)]
        for core in range(2)
        for loc in range(LOCS)
    ]


def loc_groups():
    return [[shard * LOCS + loc for loc in LOC_ORDER] for shard in range(SHARDS)]


def start_all(pairs, sems):
    copies = [pltpu.make_async_copy(a, b, sems.at[n]) for n, (a, b) in enumerate(pairs)]
    for copy in copies:
        copy.start()
    return copies


def pack(pos_hbm, q_hbm, k_hbm, v_hbm, out_hbm, pos_ref, q_ref, k_ref, v_ref, out_ref, sems, out_sems):
    copies = start_all([(pos_hbm, pos_ref), (q_hbm, q_ref), (k_hbm, k_ref), (v_hbm, v_ref)], sems)
    for copy in copies[:2]:
        copy.wait()

    wide = (PAD, HEADS_HERE * HEAD_DIM)
    to, source = iota((PAD, ROWS), 0), iota((PAD, ROWS), 1)
    place = to % TILE
    queries = pick((source == to // TILE * RUN + place) & (place < RUN), q_ref[...])
    first = (pos_ref[0] // RUN).astype(f32)
    second = (pos_ref[RUN] // RUN).astype(f32)
    numbers = jnp.where(iota(wide, 1) % HEAD_DIM < HEAD_DIM // 2, first, second)
    queries = jnp.where(iota(wide, 0) % TILE == RUN, numbers, queries).astype(bf16)

    for copy in copies[2:]:
        copy.wait()
    to, source = iota((CHUNKS * TILE, ROWS), 0), iota((CHUNKS * TILE, ROWS), 1)
    place = to % TILE
    row = to // TILE * CHUNK + place % CHUNK
    both = pick((source == row) & (place < CHUNK), k_ref[...])
    both = (both + pick((source == row) & (place >= CHUNK), v_ref[...])).astype(bf16)
    sent = []
    for z in range(RUNS * CHUNKS):
        i, j = z // CHUNKS, z % CHUNKS
        for h in range(HEADS_HERE):
            cols = slice(h * HEAD_DIM, (h + 1) * HEAD_DIM)
            out_ref[z * HEADS_HERE + h, 0:TILE, :] = queries[i * TILE : (i + 1) * TILE, cols]
            out_ref[z * HEADS_HERE + h, TILE : 2 * TILE, :] = both[j * TILE : (j + 1) * TILE, cols]
        mine = pl.ds(z * HEADS_HERE, HEADS_HERE)
        sent.append(pltpu.make_async_copy(out_ref.at[mine], out_hbm.at[mine], out_sems.at[z]))
        sent[-1].start()
    for copy in sent:
        copy.wait()


def pack_embed(e_ref, gain_ref, own_out, first_out, second_out):
    height, rows = LOCS * 2 * PAD, ROWS * PATCH
    to, source = iota((height, rows), 0), iota((height, rows), 1)
    place = to % TILE
    patch = to // TILE % RUNS * RUN + place
    slot = (to // (2 * PAD) ^ lax.axis_index("loc")) * 2 + to // PAD % 2
    moved = pick((source == patch * PATCH + slot) & (place < RUN), e_ref[...])
    high, middle, low = three_parts(gain_ref[...])
    row = iota((height, COLS), 0) % (2 * PAD)
    moved = jnp.where(row == RUN, high, moved)
    moved = jnp.where(row == TILE + RUN, middle, moved)
    moved = jnp.where(row == PAD + RUN, low, moved).astype(bf16)
    step = [moved[n * 2 * PAD : (n + 1) * 2 * PAD, :] for n in range(LOCS)]
    own_out[...] = step[0]
    first_out[0, :, :] = step[3]
    first_out[1, :, :] = step[2]
    second_out[...] = step[1]


def split(in_ref, out_ref):
    both = in_ref[:, TILE : 2 * TILE, :].astype(f32)
    out_ref[0:KN, :] = both[:, 0:CHUNK, :].reshape(KN, HEAD_DIM).astype(bf16)
    out_ref[KN : 2 * KN, :] = both[:, CHUNK:TILE, :].reshape(KN, HEAD_DIM).astype(bf16)
    numbers = in_ref[:, 0:TILE, :].astype(f32)[:, RUN:TILE, :]
    out_ref[2 * KN : 2 * KN + PEERS, :] = numbers.reshape(PEERS, HEAD_DIM).astype(bf16)


def run_starts(numbers):
    other = pltpu.roll(numbers, HEAD_DIM // 2, 1)
    lower = iota(numbers.shape, 1) < HEAD_DIM // 2
    return jnp.where(lower, numbers, other) * RUN, jnp.where(lower, other, numbers) * RUN


def key_positions(numbers, chunk):
    spot = iota((PEERS, KN), 1) // CHUNK == iota((PEERS, KN), 0)
    spot = jnp.where(spot, f32(1), f32(0)).astype(bf16)
    both = lax.dot_general(
        numbers, spot, (((0,), (0,)), ((), ())), preferred_element_type=f32
    )
    half = HEAD_DIM // 2
    first, second = both[0:8, :] * RUN, both[half : half + 8, :] * RUN
    row = iota((8, KN), 1) % CHUNK + chunk * CHUNK
    place = row.astype(f32)
    pos = jnp.where(row < RUN, first + place, second + (place - RUN))
    return jnp.where(row < ROWS, pos, f32(FAR))[0:1, :]


def attend(in_ref, kv_ref, out_hbm, out_ref, s_ref, sems):
    scale = math.log2(math.e) / math.sqrt(HEAD_DIM)
    z = lax.axis_index("za") * 4 + lax.axis_index("zb") * 2 + lax.axis_index("zc")
    place = sum(jnp.where(z == there, n, 0) for n, there in enumerate(DEPTH_ORDER))
    run, chunk = place // CHUNKS, place % CHUNKS
    key_pos, values = [], []
    for core in range(2):
        key_pos.append(key_positions(kv_ref[core, 2 * KN : 2 * KN + PEERS, :], chunk))
        ones = jnp.ones((KN, HEAD_DIM), bf16)
        values.append(jnp.concatenate([kv_ref[core, KN : 2 * KN, :], ones], axis=1))
    numbers = in_ref[:, 0:TILE, :].astype(f32)[:, RUN:TILE, :].reshape(PEERS, HEAD_DIM)
    first, second = run_starts(numbers)
    start = jnp.where(run == 0, first, second)
    blocks = STEP // TILE
    line = iota((blocks, TILE, HEAD_DIM), 1)
    lane = iota((blocks, TILE, HEAD_DIM), 2)
    own = (lane % TILE == line) & (lane < 3 * TILE)
    side = iota((blocks, HEAD_DIM), 1) // TILE
    copies = KN // HEAD_DIM
    sent = []
    for t in range(QN // STEP):
        tile = slice(t * blocks, (t + 1) * blocks)
        queries = in_ref[tile, 0:TILE, :].reshape(STEP, HEAD_DIM)
        pos = jnp.broadcast_to(start[tile, None, :], line.shape) + line.astype(f32)
        pos = jnp.where(line < RUN, pos, f32(-1)).reshape(STEP, HEAD_DIM)
        pos = jnp.concatenate([pos] * copies, axis=1)
        best = jnp.full((STEP, HEAD_DIM), FLOOR, f32)
        for core in range(2):
            scores = lax.dot_general(
                queries, kv_ref[core, 0:KN, :], (((1,), (1,)), ((), ())), preferred_element_type=f32
            )
            scores = jnp.where(key_pos[core] <= pos, scores * scale, f32(MASKED))
            s_ref[core, :, :] = scores
            for n in range(copies):
                best = jnp.maximum(best, scores[:, n * HEAD_DIM : (n + 1) * HEAD_DIM])
        best = jnp.broadcast_to(jnp.max(best, axis=1, keepdims=True), best.shape)
        wide = jnp.concatenate([best] * copies, axis=1)
        acc = jnp.zeros((STEP, 2 * HEAD_DIM), f32)
        for core in range(2):
            weights = jnp.exp2(s_ref[core, :, :] - wide).astype(bf16)
            acc = acc + jnp.dot(weights, values[core], preferred_element_type=f32)
        total = jnp.maximum(acc[:, HEAD_DIM:], f32(1e-30))
        result = (acc[:, 0:HEAD_DIM] / total).reshape(line.shape)
        best = jnp.sum(jnp.where(own, best.reshape(own.shape), f32(0)), axis=1)
        total = jnp.sum(jnp.where(own, total.reshape(own.shape), f32(0)), axis=1)
        level = best + jnp.log(jnp.maximum(total, f32(1e-30))) * math.log2(math.e)
        high, middle, low = three_parts(level)
        level = jnp.where(side == 0, high, jnp.where(side == 1, middle, low))
        level = jnp.where(side < 3, level, f32(0))
        level = jnp.broadcast_to(level[:, None, :], line.shape)
        out_ref[tile, :, :] = jnp.where(line < RUN, result, level).astype(bf16)
        for depth in range(t * blocks // PLANE, (t + 1) * blocks // PLANE):
            mine = out_ref.at[pl.ds(depth * PLANE, PLANE)]
            home = out_hbm.at[pl.ds(HOME_PLACE[depth] * PLANE, PLANE)]
            sent.append(pltpu.make_async_copy(mine, home, sems.at[depth]))
            sent[-1].start()
    for copy in sent:
        copy.wait()


def finish(part_ref, w_ref, own_ref, first_ref, second_ref, out_ref, e_ref):
    arrived = (own_ref[...], second_ref[0, :, :], second_ref[1, :, :], first_ref[0, :, :])
    for step, block in enumerate(arrived):
        origin = lax.axis_index("loc") ^ step
        e_ref[:, pl.ds(pl.multiple_of(origin * COLS, COLS), COLS)] = block
    levels = part_ref[...].astype(f32)[:, RUN:TILE, :].reshape(PEERS, HEAD_DIM)
    levels = levels + pltpu.roll(levels, 128 - TILE, 1) + pltpu.roll(levels, 128 - 2 * TILE, 1)
    levels = jnp.concatenate(
        [levels[at * PLANE : (at + 1) * PLANE, :] for at in HOME_PLACE], axis=0
    ).reshape(RUNS, CHUNKS, HEADS_HERE, 128)
    levels = jnp.exp2(levels - jnp.max(levels, axis=1, keepdims=True))
    shares = levels / jnp.sum(levels, axis=1, keepdims=True)
    shares = jnp.concatenate(
        [shares.reshape(PEERS, 128), jnp.zeros((128 - PEERS, 128), f32)], axis=0
    ).T
    real = iota((TILE, HEAD_DIM), 0) < RUN
    per_slot = SLOT_D // HEAD_DIM
    rows = []
    for u in range(2):
        for i in range(RUNS):
            heads = []
            for h in range(u * per_slot, (u + 1) * per_slot):
                acc = jnp.zeros((TILE, HEAD_DIM), f32)
                for j in range(CHUNKS):
                    block = (i * CHUNKS + j) * HEADS_HERE + h
                    partial = part_ref[HOME_PLACE[block // PLANE] * PLANE + h, :, :].astype(f32)
                    acc = acc + shares[0:TILE, block : block + 1] * partial
                heads.append(jnp.where(real, acc, f32(0)).astype(bf16))
            rows.append(jnp.concatenate(heads, axis=1))
    slots = jnp.concatenate(rows, axis=0)
    embed = e_ref[...].astype(f32)
    gain = embed[RUN : RUN + 1, :] + embed[TILE + RUN : TILE + RUN + 1, :] + embed[PAD + RUN : PAD + RUN + 1, :]
    mixed = jnp.dot(slots, w_ref[...], preferred_element_type=f32) + embed
    spread = jnp.sum(mixed * mixed, axis=1, keepdims=True) / LOCAL_D + 1e-05
    normed = (mixed / jnp.sqrt(spread) * gain).astype(bf16)
    for part in range(LOCS):
        out_ref[LOC_ORDER.index(part), :, :] = normed[:, part * COLS : (part + 1) * COLS]


def unpack(in_ref, out_ref):
    height, rows = LOCS * 2 * PAD, ROWS * PATCH
    to, source = iota((rows, height), 0), iota((rows, height), 1)
    patch = to // PATCH
    row = to % PATCH * PAD + patch // RUN * TILE + patch % RUN
    arrived = jnp.concatenate([in_ref[LOC_ORDER.index(loc), :, :] for loc in range(LOCS)], axis=0)
    moved = pick(source == row, arrived)
    out_ref[...] = moved.astype(bf16)


def vmem(count):
    return [pl.BlockSpec(memory_space=pltpu.VMEM)] * count


def call(kernel, outs, specs, scratch=(), flops=0, moved=0, limit=40 * 1024 * 1024, to_hbm=False):
    space = pltpu.HBM if to_hbm else pltpu.VMEM
    return pl.pallas_call(
        kernel,
        out_shape=outs,
        in_specs=specs,
        out_specs=jax.tree.map(lambda _: pl.BlockSpec(memory_space=space), outs),
        scratch_shapes=scratch,
        compiler_params=pltpu.CompilerParams(vmem_limit_bytes=limit),
        cost_estimate=pl.CostEstimate(flops=flops, bytes_accessed=moved, transcendentals=0),
        name=kernel.__name__,
    )


def shape(*dims):
    return jax.ShapeDtypeStruct(dims, bf16)


def swapped(block, step):
    return lax.ppermute(block, "loc", [(i, i ^ step) for i in range(LOCS)])


def on_device(queries, keys, values, positions, byte_embed, w_slot, gain):
    wide = (ROWS, HEADS_HERE * HEAD_DIM)
    messages = (PEERS, 2 * TILE, HEAD_DIM)
    results = (PEERS, TILE, HEAD_DIM)
    sent = call(
        pack,
        shape(*messages),
        [pl.BlockSpec(memory_space=pltpu.HBM)] * 4,
        [
            pltpu.SMEM((ROWS,), jnp.int32),
            pltpu.VMEM(wide, bf16),
            pltpu.VMEM(wide, bf16),
            pltpu.VMEM(wide, bf16),
            pltpu.VMEM(messages, bf16),
            pltpu.SemaphoreType.DMA((4,)),
            pltpu.SemaphoreType.DMA((RUNS * CHUNKS,)),
        ],
        limit=None,
        to_hbm=True,
    )(positions, queries, keys, values)
    sent, byte_embed = lax.optimization_barrier((sent, byte_embed))
    held = exchange(sent, seq_groups(DEPTH_ORDER))
    own, first, second = call(
        pack_embed,
        [shape(2 * PAD, COLS), shape(2, 2 * PAD, COLS), shape(2 * PAD, COLS)],
        vmem(2),
    )(byte_embed, gain.reshape(1, COLS))
    held, first = lax.optimization_barrier((held, swapped(first, 3)))
    kv = call(split, shape(2 * KN + PEERS, HEAD_DIM), vmem(1))(held)
    kv = lax.all_gather(kv, "c", axis=0, tiled=False)
    partial = call(
        attend,
        shape(*results),
        vmem(2),
        [
            pltpu.VMEM(results, bf16),
            pltpu.VMEM((2, STEP, KN), f32),
            pltpu.SemaphoreType.DMA((DEPTH,)),
        ],
        flops=4 * QN * 2 * KN * HEAD_DIM,
        moved=2 * 4 * KN * HEAD_DIM,
        to_hbm=True,
    )(held, kv)
    partial, first, second = lax.optimization_barrier((partial, first, second))
    second = swapped(jnp.stack([second, first[1]]), 1)
    partial = exchange(partial, seq_groups(HOME_ORDER))
    normed = call(
        finish,
        shape(LOCS, 2 * PAD, COLS),
        vmem(5),
        [pltpu.VMEM((2 * PAD, LOCAL_D), bf16)],
    )(partial, w_slot, own, first, second)
    columns = exchange(normed, loc_groups())
    return call(unpack, shape(ROWS * PATCH, COLS), vmem(1))(columns)


def solution(mesh):
    devices = mesh.devices.reshape(2, 2, 2, 4, 2, 2, LOCS)
    finer = Mesh(devices, SEQ + ("loc",))
    placed = (
        P(SEQ, "loc"),
        P(SEQ, "loc"),
        P(SEQ, "loc"),
        P(SEQ),
        P(SEQ, "loc"),
        P(),
        P("loc"),
    )
    return jax.shard_map(
        on_device, mesh=finer, in_specs=placed, out_specs=P(SEQ, "loc"), check_vma=False
    )
```

```python
import math

import jax
import jax.numpy as jnp
from jax import lax
from jax.experimental import pallas as pl
from jax.experimental.pallas import tpu as pltpu
from jax.sharding import Mesh
from jax.sharding import PartitionSpec as P

HEAD_DIM = 128
PATCH = 8
RUN = 15
RUNS = 2
ROWS = RUN * RUNS
TILE = 16
PAD = RUNS * TILE
CHUNK = 8
CHUNKS = 4
HEADS_HERE = 8
LOCAL_D = 1024
SLOT_D = 512
LOCS = 4
COLS = LOCAL_D // LOCS
SEQ = ("za", "zb", "zc", "x", "yl", "c")
EVERY = SEQ + ("loc",)
DEPTH, PLANE = 8, 8
DEPTH_ORDER = (7, 3, 1, 5, 6, 2, 0, 4)
HOME_ORDER = (7, 2, 4, 3, 5, 0, 6, 1)
HOME_PLACE = tuple(HOME_ORDER.index(z) for z in DEPTH_ORDER)
LOC_ORDER = (2, 0, 1, 3)
SHARDS = DEPTH * PLANE * 2
PEERS = RUNS * CHUNKS * HEADS_HERE
QN = PEERS * TILE
KN = PEERS * CHUNK
STEP = 256
FLOOR = -1e20
MASKED = -1e30
FAR = 1e6
bf16 = jnp.bfloat16
f32 = jnp.float32


def iota(shape, dim):
    return lax.broadcasted_iota(jnp.int32, shape, dim)


def pick(condition, rows):
    select = jnp.where(condition, f32(1), f32(0)).astype(bf16)
    return jnp.dot(select, rows, preferred_element_type=f32)


def three_parts(x):
    high = x.astype(bf16).astype(f32)
    middle = (x - high).astype(bf16).astype(f32)
    return high, middle, x - high - middle


def exchange(blocks, groups):
    return lax.all_to_all(
        blocks, EVERY, split_axis=0, concat_axis=0, tiled=True, axis_index_groups=groups
    )


def seq_groups(depth_order):
    return [
        [((z * PLANE + spot) * 2 + core) * LOCS + loc for z in depth_order for spot in range(PLANE)]
        for core in range(2)
        for loc in range(LOCS)
    ]


def loc_groups():
    return [[shard * LOCS + loc for loc in LOC_ORDER] for shard in range(SHARDS)]


def start_all(pairs, sems):
    copies = [pltpu.make_async_copy(a, b, sems.at[n]) for n, (a, b) in enumerate(pairs)]
    for copy in copies:
        copy.start()
    return copies


def pack(pos_hbm, q_hbm, k_hbm, v_hbm, out_hbm, pos_ref, q_ref, k_ref, v_ref, out_ref, sems, out_sems):
    copies = start_all([(pos_hbm, pos_ref), (q_hbm, q_ref), (k_hbm, k_ref), (v_hbm, v_ref)], sems)
    for copy in copies[:2]:
        copy.wait()

    wide = (PAD, HEADS_HERE * HEAD_DIM)
    to, source = iota((PAD, ROWS), 0), iota((PAD, ROWS), 1)
    place = to % TILE
    queries = pick((source == to // TILE * RUN + place) & (place < RUN), q_ref[...])
    first = (pos_ref[0] // RUN).astype(f32)
    second = (pos_ref[RUN] // RUN).astype(f32)
    numbers = jnp.where(iota(wide, 1) % HEAD_DIM < HEAD_DIM // 2, first, second)
    queries = jnp.where(iota(wide, 0) % TILE == RUN, numbers, queries).astype(bf16)

    for copy in copies[2:]:
        copy.wait()
    to, source = iota((CHUNKS * TILE, ROWS), 0), iota((CHUNKS * TILE, ROWS), 1)
    place = to % TILE
    row = to // TILE * CHUNK + place % CHUNK
    both = pick((source == row) & (place < CHUNK), k_ref[...])
    both = (both + pick((source == row) & (place >= CHUNK), v_ref[...])).astype(bf16)
    sent = []
    for z in range(RUNS * CHUNKS):
        i, j = z // CHUNKS, z % CHUNKS
        for h in range(HEADS_HERE):
            cols = slice(h * HEAD_DIM, (h + 1) * HEAD_DIM)
            out_ref[z * HEADS_HERE + h, 0:TILE, :] = queries[i * TILE : (i + 1) * TILE, cols]
            out_ref[z * HEADS_HERE + h, TILE : 2 * TILE, :] = both[j * TILE : (j + 1) * TILE, cols]
        mine = pl.ds(z * HEADS_HERE, HEADS_HERE)
        sent.append(pltpu.make_async_copy(out_ref.at[mine], out_hbm.at[mine], out_sems.at[z]))
        sent[-1].start()
    for copy in sent:
        copy.wait()


def pack_embed(e_ref, gain_ref, own_out, first_out, second_out):
    height, rows = LOCS * 2 * PAD, ROWS * PATCH
    to, source = iota((height, rows), 0), iota((height, rows), 1)
    place = to % TILE
    patch = to // TILE % RUNS * RUN + place
    slot = (to // (2 * PAD) ^ lax.axis_index("loc")) * 2 + to // PAD % 2
    moved = pick((source == patch * PATCH + slot) & (place < RUN), e_ref[...])
    high, middle, low = three_parts(gain_ref[...])
    row = iota((height, COLS), 0) % (2 * PAD)
    moved = jnp.where(row == RUN, high, moved)
    moved = jnp.where(row == TILE + RUN, middle, moved)
    moved = jnp.where(row == PAD + RUN, low, moved).astype(bf16)
    step = [moved[n * 2 * PAD : (n + 1) * 2 * PAD, :] for n in range(LOCS)]
    own_out[...] = step[0]
    first_out[0, :, :] = step[3]
    first_out[1, :, :] = step[2]
    second_out[...] = step[1]


def split(in_ref, out_ref):
    both = in_ref[:, TILE : 2 * TILE, :].astype(f32)
    out_ref[0:KN, :] = both[:, 0:CHUNK, :].reshape(KN, HEAD_DIM).astype(bf16)
    out_ref[KN : 2 * KN, :] = both[:, CHUNK:TILE, :].reshape(KN, HEAD_DIM).astype(bf16)
    numbers = in_ref[:, 0:TILE, :].astype(f32)[:, RUN:TILE, :]
    out_ref[2 * KN : 2 * KN + PEERS, :] = numbers.reshape(PEERS, HEAD_DIM).astype(bf16)


def run_starts(numbers):
    other = pltpu.roll(numbers, HEAD_DIM // 2, 1)
    lower = iota(numbers.shape, 1) < HEAD_DIM // 2
    return jnp.where(lower, numbers, other) * RUN, jnp.where(lower, other, numbers) * RUN


def key_positions(numbers, chunk):
    spot = iota((PEERS, KN), 1) // CHUNK == iota((PEERS, KN), 0)
    spot = jnp.where(spot, f32(1), f32(0)).astype(bf16)
    both = lax.dot_general(
        numbers, spot, (((0,), (0,)), ((), ())), preferred_element_type=f32
    )
    half = HEAD_DIM // 2
    first, second = both[0:8, :] * RUN, both[half : half + 8, :] * RUN
    row = iota((8, KN), 1) % CHUNK + chunk * CHUNK
    place = row.astype(f32)
    pos = jnp.where(row < RUN, first + place, second + (place - RUN))
    return jnp.where(row < ROWS, pos, f32(FAR))[0:1, :]


def attend(in_ref, kv_ref, out_hbm, out_ref, s_ref, sems):
    scale = math.log2(math.e) / math.sqrt(HEAD_DIM)
    z = lax.axis_index("za") * 4 + lax.axis_index("zb") * 2 + lax.axis_index("zc")
    place = sum(jnp.where(z == there, n, 0) for n, there in enumerate(DEPTH_ORDER))
    run, chunk = place // CHUNKS, place % CHUNKS
    key_pos, values = [], []
    for core in range(2):
        key_pos.append(key_positions(kv_ref[core, 2 * KN : 2 * KN + PEERS, :], chunk))
        ones = jnp.ones((KN, HEAD_DIM), bf16)
        values.append(jnp.concatenate([kv_ref[core, KN : 2 * KN, :], ones], axis=1))
    numbers = in_ref[:, 0:TILE, :].astype(f32)[:, RUN:TILE, :].reshape(PEERS, HEAD_DIM)
    first, second = run_starts(numbers)
    start = jnp.where(run == 0, first, second)
    blocks = STEP // TILE
    line = iota((blocks, TILE, HEAD_DIM), 1)
    lane = iota((blocks, TILE, HEAD_DIM), 2)
    own = (lane % TILE == line) & (lane < 3 * TILE)
    side = iota((blocks, HEAD_DIM), 1) // TILE
    copies = KN // HEAD_DIM
    sent = []
    for t in range(QN // STEP):
        tile = slice(t * blocks, (t + 1) * blocks)
        queries = in_ref[tile, 0:TILE, :].reshape(STEP, HEAD_DIM)
        pos = jnp.broadcast_to(start[tile, None, :], line.shape) + line.astype(f32)
        pos = jnp.where(line < RUN, pos, f32(-1)).reshape(STEP, HEAD_DIM)
        pos = jnp.concatenate([pos] * copies, axis=1)
        best = jnp.full((STEP, HEAD_DIM), FLOOR, f32)
        for core in range(2):
            scores = lax.dot_general(
                queries, kv_ref[core, 0:KN, :], (((1,), (1,)), ((), ())), preferred_element_type=f32
            )
            scores = jnp.where(key_pos[core] <= pos, scores * scale, f32(MASKED))
            s_ref[core, :, :] = scores
            for n in range(copies):
                best = jnp.maximum(best, scores[:, n * HEAD_DIM : (n + 1) * HEAD_DIM])
        best = jnp.broadcast_to(jnp.max(best, axis=1, keepdims=True), best.shape)
        wide = jnp.concatenate([best] * copies, axis=1)
        acc = jnp.zeros((STEP, 2 * HEAD_DIM), f32)
        for core in range(2):
            weights = jnp.exp2(s_ref[core, :, :] - wide).astype(bf16)
            acc = acc + jnp.dot(weights, values[core], preferred_element_type=f32)
        total = jnp.maximum(acc[:, HEAD_DIM:], f32(1e-30))
        result = (acc[:, 0:HEAD_DIM] / total).reshape(line.shape)
        best = jnp.sum(jnp.where(own, best.reshape(own.shape), f32(0)), axis=1)
        total = jnp.sum(jnp.where(own, total.reshape(own.shape), f32(0)), axis=1)
        level = best + jnp.log(jnp.maximum(total, f32(1e-30))) * math.log2(math.e)
        high, middle, low = three_parts(level)
        level = jnp.where(side == 0, high, jnp.where(side == 1, middle, low))
        level = jnp.where(side < 3, level, f32(0))
        level = jnp.broadcast_to(level[:, None, :], line.shape)
        out_ref[tile, :, :] = jnp.where(line < RUN, result, level).astype(bf16)
        for depth in range(t * blocks // PLANE, (t + 1) * blocks // PLANE):
            mine = out_ref.at[pl.ds(depth * PLANE, PLANE)]
            home = out_hbm.at[pl.ds(HOME_PLACE[depth] * PLANE, PLANE)]
            sent.append(pltpu.make_async_copy(mine, home, sems.at[depth]))
            sent[-1].start()
    for copy in sent:
        copy.wait()


def finish(part_ref, w_ref, own_ref, first_ref, second_ref, out_ref, e_ref):
    arrived = (own_ref[...], second_ref[0, :, :], second_ref[1, :, :], first_ref[0, :, :])
    for step, block in enumerate(arrived):
        origin = lax.axis_index("loc") ^ step
        e_ref[:, pl.ds(pl.multiple_of(origin * COLS, COLS), COLS)] = block
    levels = part_ref[...].astype(f32)[:, RUN:TILE, :].reshape(PEERS, HEAD_DIM)
    levels = levels + pltpu.roll(levels, 128 - TILE, 1) + pltpu.roll(levels, 128 - 2 * TILE, 1)
    levels = jnp.concatenate(
        [levels[at * PLANE : (at + 1) * PLANE, :] for at in HOME_PLACE], axis=0
    ).reshape(RUNS, CHUNKS, HEADS_HERE, 128)
    levels = jnp.exp2(levels - jnp.max(levels, axis=1, keepdims=True))
    shares = levels / jnp.sum(levels, axis=1, keepdims=True)
    shares = jnp.concatenate(
        [shares.reshape(PEERS, 128), jnp.zeros((128 - PEERS, 128), f32)], axis=0
    ).T
    real = iota((TILE, HEAD_DIM), 0) < RUN
    per_slot = SLOT_D // HEAD_DIM
    rows = []
    for u in range(2):
        for i in range(RUNS):
            heads = []
            for h in range(u * per_slot, (u + 1) * per_slot):
                acc = jnp.zeros((TILE, HEAD_DIM), f32)
                for j in range(CHUNKS):
                    block = (i * CHUNKS + j) * HEADS_HERE + h
                    partial = part_ref[HOME_PLACE[block // PLANE] * PLANE + h, :, :].astype(f32)
                    acc = acc + shares[0:TILE, block : block + 1] * partial
                heads.append(jnp.where(real, acc, f32(0)).astype(bf16))
            rows.append(jnp.concatenate(heads, axis=1))
    slots = jnp.concatenate(rows, axis=0)
    embed = e_ref[...].astype(f32)
    gain = embed[RUN : RUN + 1, :] + embed[TILE + RUN : TILE + RUN + 1, :] + embed[PAD + RUN : PAD + RUN + 1, :]
    mixed = jnp.dot(slots, w_ref[...], preferred_element_type=f32) + embed
    spread = jnp.sum(mixed * mixed, axis=1, keepdims=True) / LOCAL_D + 1e-05
    normed = (mixed / jnp.sqrt(spread) * gain).astype(bf16)
    for part in range(LOCS):
        out_ref[LOC_ORDER.index(part), :, :] = normed[:, part * COLS : (part + 1) * COLS]


def unpack(in_ref, out_ref):
    height, rows = LOCS * 2 * PAD, ROWS * PATCH
    to, source = iota((rows, height), 0), iota((rows, height), 1)
    patch = to // PATCH
    row = to % PATCH * PAD + patch // RUN * TILE + patch % RUN
    arrived = jnp.concatenate([in_ref[LOC_ORDER.index(loc), :, :] for loc in range(LOCS)], axis=0)
    moved = pick(source == row, arrived)
    out_ref[...] = moved.astype(bf16)


def vmem(count):
    return [pl.BlockSpec(memory_space=pltpu.VMEM)] * count


def call(kernel, outs, specs, scratch=(), flops=0, moved=0, limit=40 * 1024 * 1024, to_hbm=False):
    space = pltpu.HBM if to_hbm else pltpu.VMEM
    return pl.pallas_call(
        kernel,
        out_shape=outs,
        in_specs=specs,
        out_specs=jax.tree.map(lambda _: pl.BlockSpec(memory_space=space), outs),
        scratch_shapes=scratch,
        compiler_params=pltpu.CompilerParams(vmem_limit_bytes=limit),
        cost_estimate=pl.CostEstimate(flops=flops, bytes_accessed=moved, transcendentals=0),
        name=kernel.__name__,
    )


def shape(*dims):
    return jax.ShapeDtypeStruct(dims, bf16)


def swapped(block, step):
    return lax.ppermute(block, "loc", [(i, i ^ step) for i in range(LOCS)])


def on_device(queries, keys, values, positions, byte_embed, w_slot, gain):
    wide = (ROWS, HEADS_HERE * HEAD_DIM)
    messages = (PEERS, 2 * TILE, HEAD_DIM)
    results = (PEERS, TILE, HEAD_DIM)
    sent = call(
        pack,
        shape(*messages),
        [pl.BlockSpec(memory_space=pltpu.HBM)] * 4,
        [
            pltpu.SMEM((ROWS,), jnp.int32),
            pltpu.VMEM(wide, bf16),
            pltpu.VMEM(wide, bf16),
            pltpu.VMEM(wide, bf16),
            pltpu.VMEM(messages, bf16),
            pltpu.SemaphoreType.DMA((4,)),
            pltpu.SemaphoreType.DMA((RUNS * CHUNKS,)),
        ],
        limit=None,
        to_hbm=True,
    )(positions, queries, keys, values)
    sent, byte_embed = lax.optimization_barrier((sent, byte_embed))
    held = exchange(sent, seq_groups(DEPTH_ORDER))
    own, first, second = call(
        pack_embed,
        [shape(2 * PAD, COLS), shape(2, 2 * PAD, COLS), shape(2 * PAD, COLS)],
        vmem(2),
    )(byte_embed, gain.reshape(1, COLS))
    held, first = lax.optimization_barrier((held, swapped(first, 3)))
    kv = call(split, shape(2 * KN + PEERS, HEAD_DIM), vmem(1))(held)
    kv = lax.all_gather(kv, "c", axis=0, tiled=False)
    partial = call(
        attend,
        shape(*results),
        vmem(2),
        [
            pltpu.VMEM(results, bf16),
            pltpu.VMEM((2, STEP, KN), f32),
            pltpu.SemaphoreType.DMA((DEPTH,)),
        ],
        flops=4 * QN * 2 * KN * HEAD_DIM,
        moved=2 * 4 * KN * HEAD_DIM,
        to_hbm=True,
    )(held, kv)
    partial, first, second = lax.optimization_barrier((partial, first, second))
    second = swapped(jnp.stack([second, first[1]]), 1)
    partial = exchange(partial, seq_groups(HOME_ORDER))
    normed = call(
        finish,
        shape(LOCS, 2 * PAD, COLS),
        vmem(5),
        [pltpu.VMEM((2 * PAD, LOCAL_D), bf16)],
    )(partial, w_slot, own, first, second)
    columns = exchange(normed, loc_groups())
    return call(unpack, shape(ROWS * PATCH, COLS), vmem(1))(columns)


def solution(mesh):
    devices = mesh.devices.reshape(2, 2, 2, 4, 2, 2, LOCS)
    finer = Mesh(devices, SEQ + ("loc",))
    placed = (
        P(SEQ, "loc"),
        P(SEQ, "loc"),
        P(SEQ, "loc"),
        P(SEQ),
        P(SEQ, "loc"),
        P(),
        P("loc"),
    )
    return jax.shard_map(
        on_device, mesh=finer, in_specs=placed, out_specs=P(SEQ, "loc"), check_vma=False
    )
```

```python
import math

import jax
import jax.numpy as jnp
from jax import lax
from jax.experimental import pallas as pl
from jax.experimental.pallas import tpu as pltpu
from jax.sharding import Mesh
from jax.sharding import PartitionSpec as P

HEAD_DIM = 128
PATCH = 8
RUN = 15
RUNS = 2
ROWS = RUN * RUNS
TILE = 16
PAD = RUNS * TILE
CHUNK = 8
CHUNKS = 4
HEADS_HERE = 8
LOCAL_D = 1024
SLOT_D = 512
LOCS = 4
COLS = LOCAL_D // LOCS
SEQ = ("za", "zb", "zc", "x", "yl", "c")
EVERY = SEQ + ("loc",)
DEPTH, PLANE = 8, 8
DEPTH_ORDER = (7, 3, 1, 5, 6, 2, 0, 4)
HOME_ORDER = (7, 2, 4, 3, 5, 0, 6, 1)
HOME_PLACE = tuple(HOME_ORDER.index(z) for z in DEPTH_ORDER)
LOC_ORDER = (2, 0, 1, 3)
SHARDS = DEPTH * PLANE * 2
PEERS = RUNS * CHUNKS * HEADS_HERE
QN = PEERS * TILE
KN = PEERS * CHUNK
STEP = 256
FLOOR = -1e20
MASKED = -1e30
FAR = 1e6
bf16 = jnp.bfloat16
f32 = jnp.float32


def iota(shape, dim):
    return lax.broadcasted_iota(jnp.int32, shape, dim)


def picker(condition):
    return jnp.where(condition, f32(1), f32(0)).astype(bf16)


def pick(condition, rows):
    return jnp.dot(picker(condition), rows, preferred_element_type=f32)


def three_parts(x):
    high = x.astype(bf16).astype(f32)
    middle = (x - high).astype(bf16).astype(f32)
    return high, middle, x - high - middle


def exchange(blocks, groups):
    return lax.all_to_all(
        blocks, EVERY, split_axis=0, concat_axis=0, tiled=True, axis_index_groups=groups
    )


def seq_groups(depth_order):
    return [
        [((z * PLANE + spot) * 2 + core) * LOCS + loc for z in depth_order for spot in range(PLANE)]
        for core in range(2)
        for loc in range(LOCS)
    ]


def loc_groups():
    return [[shard * LOCS + loc for loc in LOC_ORDER] for shard in range(SHARDS)]


def start_all(pairs, sems):
    copies = [pltpu.make_async_copy(a, b, sems.at[n]) for n, (a, b) in enumerate(pairs)]
    for copy in copies:
        copy.start()
    return copies


def pack(pos_hbm, q_hbm, k_hbm, v_hbm, out_hbm, pos_ref, q_ref, k_ref, v_ref, out_ref, sems, out_sems):
    copies = start_all([(pos_hbm, pos_ref), (q_hbm, q_ref), (k_hbm, k_ref), (v_hbm, v_ref)], sems)
    wide = (PAD, HEADS_HERE * HEAD_DIM)
    to, source = iota((PAD, ROWS), 0), iota((PAD, ROWS), 1)
    place = to % TILE
    pick_queries = picker((source == to // TILE * RUN + place) & (place < RUN))
    first_half = iota(wide, 1) % HEAD_DIM < HEAD_DIM // 2
    spare = iota(wide, 0) % TILE == RUN
    to, source = iota((CHUNKS * TILE, ROWS), 0), iota((CHUNKS * TILE, ROWS), 1)
    place = to % TILE
    row = to // TILE * CHUNK + place % CHUNK
    pick_keys = picker((source == row) & (place < CHUNK))
    pick_values = picker((source == row) & (place >= CHUNK))

    for copy in copies[2:]:
        copy.wait()
    both = jnp.dot(pick_keys, k_ref[...], preferred_element_type=f32)
    both = (both + jnp.dot(pick_values, v_ref[...], preferred_element_type=f32)).astype(bf16)
    for copy in copies[:2]:
        copy.wait()
    queries = jnp.dot(pick_queries, q_ref[...], preferred_element_type=f32)
    first = (pos_ref[0] // RUN).astype(f32)
    second = (pos_ref[RUN] // RUN).astype(f32)
    numbers = jnp.where(first_half, first, second)
    queries = jnp.where(spare, numbers, queries).astype(bf16)
    sent = []
    for z in range(RUNS * CHUNKS):
        i, j = z // CHUNKS, z % CHUNKS
        for h in range(HEADS_HERE):
            cols = slice(h * HEAD_DIM, (h + 1) * HEAD_DIM)
            out_ref[z * HEADS_HERE + h, 0:TILE, :] = queries[i * TILE : (i + 1) * TILE, cols]
            out_ref[z * HEADS_HERE + h, TILE : 2 * TILE, :] = both[j * TILE : (j + 1) * TILE, cols]
        mine = pl.ds(z * HEADS_HERE, HEADS_HERE)
        sent.append(pltpu.make_async_copy(out_ref.at[mine], out_hbm.at[mine], out_sems.at[z]))
        sent[-1].start()
    for copy in sent:
        copy.wait()


def pack_embed(e_ref, gain_ref, own_out, first_out, second_out):
    height, rows = LOCS * 2 * PAD, ROWS * PATCH
    to, source = iota((height, rows), 0), iota((height, rows), 1)
    place = to % TILE
    patch = to // TILE % RUNS * RUN + place
    slot = (to // (2 * PAD) ^ lax.axis_index("loc")) * 2 + to // PAD % 2
    moved = pick((source == patch * PATCH + slot) & (place < RUN), e_ref[...])
    high, middle, low = three_parts(gain_ref[...])
    row = iota((height, COLS), 0) % (2 * PAD)
    moved = jnp.where(row == RUN, high, moved)
    moved = jnp.where(row == TILE + RUN, middle, moved)
    moved = jnp.where(row == PAD + RUN, low, moved).astype(bf16)
    step = [moved[n * 2 * PAD : (n + 1) * 2 * PAD, :] for n in range(LOCS)]
    own_out[...] = step[0]
    first_out[0, :, :] = step[3]
    first_out[1, :, :] = step[2]
    second_out[...] = step[1]


def split(in_ref, out_ref):
    both = in_ref[:, TILE : 2 * TILE, :].astype(f32)
    out_ref[0:KN, :] = both[:, 0:CHUNK, :].reshape(KN, HEAD_DIM).astype(bf16)
    out_ref[KN : 2 * KN, :] = both[:, CHUNK:TILE, :].reshape(KN, HEAD_DIM).astype(bf16)
    numbers = in_ref[:, 0:TILE, :].astype(f32)[:, RUN:TILE, :]
    out_ref[2 * KN : 2 * KN + PEERS, :] = numbers.reshape(PEERS, HEAD_DIM).astype(bf16)


def run_starts(numbers):
    other = pltpu.roll(numbers, HEAD_DIM // 2, 1)
    lower = iota(numbers.shape, 1) < HEAD_DIM // 2
    return jnp.where(lower, numbers, other) * RUN, jnp.where(lower, other, numbers) * RUN


def key_positions(numbers, chunk):
    spot = iota((PEERS, KN), 1) // CHUNK == iota((PEERS, KN), 0)
    spot = jnp.where(spot, f32(1), f32(0)).astype(bf16)
    both = lax.dot_general(
        numbers, spot, (((0,), (0,)), ((), ())), preferred_element_type=f32
    )
    half = HEAD_DIM // 2
    first, second = both[0:8, :] * RUN, both[half : half + 8, :] * RUN
    row = iota((8, KN), 1) % CHUNK + chunk * CHUNK
    place = row.astype(f32)
    pos = jnp.where(row < RUN, first + place, second + (place - RUN))
    return jnp.where(row < ROWS, pos, f32(FAR))[0:1, :]


def attend(in_ref, kv_ref, out_hbm, out_ref, s_ref, sems):
    scale = math.log2(math.e) / math.sqrt(HEAD_DIM)
    z = lax.axis_index("za") * 4 + lax.axis_index("zb") * 2 + lax.axis_index("zc")
    place = sum(jnp.where(z == there, n, 0) for n, there in enumerate(DEPTH_ORDER))
    run, chunk = place // CHUNKS, place % CHUNKS
    key_pos, values = [], []
    for core in range(2):
        key_pos.append(key_positions(kv_ref[core, 2 * KN : 2 * KN + PEERS, :], chunk))
        ones = jnp.ones((KN, HEAD_DIM), bf16)
        values.append(jnp.concatenate([kv_ref[core, KN : 2 * KN, :], ones], axis=1))
    numbers = in_ref[:, 0:TILE, :].astype(f32)[:, RUN:TILE, :].reshape(PEERS, HEAD_DIM)
    first, second = run_starts(numbers)
    start = jnp.where(run == 0, first, second)
    blocks = STEP // TILE
    line = iota((blocks, TILE, HEAD_DIM), 1)
    lane = iota((blocks, TILE, HEAD_DIM), 2)
    own = (lane % TILE == line) & (lane < 3 * TILE)
    side = iota((blocks, HEAD_DIM), 1) // TILE
    copies = KN // HEAD_DIM
    sent = []
    for t in range(QN // STEP):
        tile = slice(t * blocks, (t + 1) * blocks)
        queries = in_ref[tile, 0:TILE, :].reshape(STEP, HEAD_DIM)
        pos = jnp.broadcast_to(start[tile, None, :], line.shape) + line.astype(f32)
        pos = jnp.where(line < RUN, pos, f32(-1)).reshape(STEP, HEAD_DIM)
        pos = jnp.concatenate([pos] * copies, axis=1)
        best = jnp.full((STEP, HEAD_DIM), FLOOR, f32)
        for core in range(2):
            scores = lax.dot_general(
                queries, kv_ref[core, 0:KN, :], (((1,), (1,)), ((), ())), preferred_element_type=f32
            )
            scores = jnp.where(key_pos[core] <= pos, scores * scale, f32(MASKED))
            s_ref[core, :, :] = scores
            for n in range(copies):
                best = jnp.maximum(best, scores[:, n * HEAD_DIM : (n + 1) * HEAD_DIM])
        best = jnp.broadcast_to(jnp.max(best, axis=1, keepdims=True), best.shape)
        wide = jnp.concatenate([best] * copies, axis=1)
        acc = jnp.zeros((STEP, 2 * HEAD_DIM), f32)
        for core in range(2):
            weights = jnp.exp2(s_ref[core, :, :] - wide).astype(bf16)
            acc = acc + jnp.dot(weights, values[core], preferred_element_type=f32)
        total = jnp.maximum(acc[:, HEAD_DIM:], f32(1e-30))
        result = (acc[:, 0:HEAD_DIM] / total).reshape(line.shape)
        best = jnp.sum(jnp.where(own, best.reshape(own.shape), f32(0)), axis=1)
        total = jnp.sum(jnp.where(own, total.reshape(own.shape), f32(0)), axis=1)
        level = best + jnp.log(jnp.maximum(total, f32(1e-30))) * math.log2(math.e)
        high, middle, low = three_parts(level)
        level = jnp.where(side == 0, high, jnp.where(side == 1, middle, low))
        level = jnp.where(side < 3, level, f32(0))
        level = jnp.broadcast_to(level[:, None, :], line.shape)
        out_ref[tile, :, :] = jnp.where(line < RUN, result, level).astype(bf16)
        for depth in range(t * blocks // PLANE, (t + 1) * blocks // PLANE):
            mine = out_ref.at[pl.ds(depth * PLANE, PLANE)]
            home = out_hbm.at[pl.ds(HOME_PLACE[depth] * PLANE, PLANE)]
            sent.append(pltpu.make_async_copy(mine, home, sems.at[depth]))
            sent[-1].start()
    for copy in sent:
        copy.wait()


def finish(part_ref, w_ref, own_ref, first_ref, second_ref, out_ref, e_ref):
    arrived = (own_ref[...], second_ref[0, :, :], second_ref[1, :, :], first_ref[0, :, :])
    for step, block in enumerate(arrived):
        origin = lax.axis_index("loc") ^ step
        e_ref[:, pl.ds(pl.multiple_of(origin * COLS, COLS), COLS)] = block
    levels = part_ref[...].astype(f32)[:, RUN:TILE, :].reshape(PEERS, HEAD_DIM)
    levels = levels + pltpu.roll(levels, 128 - TILE, 1) + pltpu.roll(levels, 128 - 2 * TILE, 1)
    levels = jnp.concatenate(
        [levels[at * PLANE : (at + 1) * PLANE, :] for at in HOME_PLACE], axis=0
    ).reshape(RUNS, CHUNKS, HEADS_HERE, 128)
    levels = jnp.exp2(levels - jnp.max(levels, axis=1, keepdims=True))
    shares = levels / jnp.sum(levels, axis=1, keepdims=True)
    shares = jnp.concatenate(
        [shares.reshape(PEERS, 128), jnp.zeros((128 - PEERS, 128), f32)], axis=0
    ).T
    real = iota((TILE, HEAD_DIM), 0) < RUN
    per_slot = SLOT_D // HEAD_DIM
    rows = []
    for u in range(2):
        for i in range(RUNS):
            heads = []
            for h in range(u * per_slot, (u + 1) * per_slot):
                acc = jnp.zeros((TILE, HEAD_DIM), f32)
                for j in range(CHUNKS):
                    block = (i * CHUNKS + j) * HEADS_HERE + h
                    partial = part_ref[HOME_PLACE[block // PLANE] * PLANE + h, :, :].astype(f32)
                    acc = acc + shares[0:TILE, block : block + 1] * partial
                heads.append(jnp.where(real, acc, f32(0)).astype(bf16))
            rows.append(jnp.concatenate(heads, axis=1))
    slots = jnp.concatenate(rows, axis=0)
    embed = e_ref[...].astype(f32)
    gain = embed[RUN : RUN + 1, :] + embed[TILE + RUN : TILE + RUN + 1, :] + embed[PAD + RUN : PAD + RUN + 1, :]
    mixed = jnp.dot(slots, w_ref[...], preferred_element_type=f32) + embed
    spread = jnp.sum(mixed * mixed, axis=1, keepdims=True) / LOCAL_D + 1e-05
    normed = (mixed / jnp.sqrt(spread) * gain).astype(bf16)
    for part in range(LOCS):
        out_ref[LOC_ORDER.index(part), :, :] = normed[:, part * COLS : (part + 1) * COLS]


def unpack(in_ref, out_ref):
    height, rows = LOCS * 2 * PAD, ROWS * PATCH
    to, source = iota((rows, height), 0), iota((rows, height), 1)
    patch = to // PATCH
    row = to % PATCH * PAD + patch // RUN * TILE + patch % RUN
    arrived = jnp.concatenate([in_ref[LOC_ORDER.index(loc), :, :] for loc in range(LOCS)], axis=0)
    moved = pick(source == row, arrived)
    out_ref[...] = moved.astype(bf16)


def vmem(count):
    return [pl.BlockSpec(memory_space=pltpu.VMEM)] * count


def call(kernel, outs, specs, scratch=(), flops=0, moved=0, limit=40 * 1024 * 1024, to_hbm=False):
    space = pltpu.HBM if to_hbm else pltpu.VMEM
    return pl.pallas_call(
        kernel,
        out_shape=outs,
        in_specs=specs,
        out_specs=jax.tree.map(lambda _: pl.BlockSpec(memory_space=space), outs),
        scratch_shapes=scratch,
        compiler_params=pltpu.CompilerParams(vmem_limit_bytes=limit),
        cost_estimate=pl.CostEstimate(flops=flops, bytes_accessed=moved, transcendentals=0),
        name=kernel.__name__,
    )


def shape(*dims):
    return jax.ShapeDtypeStruct(dims, bf16)


def swapped(block, step):
    return lax.ppermute(block, "loc", [(i, i ^ step) for i in range(LOCS)])


def on_device(queries, keys, values, positions, byte_embed, w_slot, gain):
    wide = (ROWS, HEADS_HERE * HEAD_DIM)
    messages = (PEERS, 2 * TILE, HEAD_DIM)
    results = (PEERS, TILE, HEAD_DIM)
    sent = call(
        pack,
        shape(*messages),
        [pl.BlockSpec(memory_space=pltpu.HBM)] * 4,
        [
            pltpu.SMEM((ROWS,), jnp.int32),
            pltpu.VMEM(wide, bf16),
            pltpu.VMEM(wide, bf16),
            pltpu.VMEM(wide, bf16),
            pltpu.VMEM(messages, bf16),
            pltpu.SemaphoreType.DMA((4,)),
            pltpu.SemaphoreType.DMA((RUNS * CHUNKS,)),
        ],
        limit=None,
        to_hbm=True,
    )(positions, queries, keys, values)
    sent, byte_embed = lax.optimization_barrier((sent, byte_embed))
    held = exchange(sent, seq_groups(DEPTH_ORDER))
    own, first, second = call(
        pack_embed,
        [shape(2 * PAD, COLS), shape(2, 2 * PAD, COLS), shape(2 * PAD, COLS)],
        vmem(2),
    )(byte_embed, gain.reshape(1, COLS))
    held, first = lax.optimization_barrier((held, swapped(first, 3)))
    kv = call(split, shape(2 * KN + PEERS, HEAD_DIM), vmem(1))(held)
    kv = lax.all_gather(kv, "c", axis=0, tiled=False)
    partial = call(
        attend,
        shape(*results),
        vmem(2),
        [
            pltpu.VMEM(results, bf16),
            pltpu.VMEM((2, STEP, KN), f32),
            pltpu.SemaphoreType.DMA((DEPTH,)),
        ],
        flops=4 * QN * 2 * KN * HEAD_DIM,
        moved=2 * 4 * KN * HEAD_DIM,
        to_hbm=True,
    )(held, kv)
    partial, first, second = lax.optimization_barrier((partial, first, second))
    second = swapped(jnp.stack([second, first[1]]), 1)
    partial = exchange(partial, seq_groups(HOME_ORDER))
    normed = call(
        finish,
        shape(LOCS, 2 * PAD, COLS),
        vmem(5),
        [pltpu.VMEM((2 * PAD, LOCAL_D), bf16)],
    )(partial, w_slot, own, first, second)
    columns = exchange(normed, loc_groups())
    return call(unpack, shape(ROWS * PATCH, COLS), vmem(1))(columns)


def solution(mesh):
    devices = mesh.devices.reshape(2, 2, 2, 4, 2, 2, LOCS)
    finer = Mesh(devices, SEQ + ("loc",))
    placed = (
        P(SEQ, "loc"),
        P(SEQ, "loc"),
        P(SEQ, "loc"),
        P(SEQ),
        P(SEQ, "loc"),
        P(),
        P("loc"),
    )
    return jax.shard_map(
        on_device, mesh=finer, in_specs=placed, out_specs=P(SEQ, "loc"), check_vma=False
    )
```

```python
import math

import jax
import jax.numpy as jnp
from jax import lax
from jax.experimental import pallas as pl
from jax.experimental.pallas import tpu as pltpu
from jax.sharding import Mesh
from jax.sharding import PartitionSpec as P

HEAD_DIM = 128
PATCH = 8
RUN = 15
RUNS = 2
ROWS = RUN * RUNS
TILE = 16
PAD = RUNS * TILE
CHUNK = 8
CHUNKS = 4
HEADS_HERE = 8
LOCAL_D = 1024
SLOT_D = 512
LOCS = 4
COLS = LOCAL_D // LOCS
SEQ = ("za", "zb", "zc", "x", "yl", "c")
EVERY = SEQ + ("loc",)
DEPTH, PLANE = 8, 8
DEPTH_ORDER = (7, 3, 1, 5, 6, 2, 0, 4)
HOME_ORDER = (7, 2, 4, 3, 5, 0, 6, 1)
HOME_PLACE = tuple(HOME_ORDER.index(z) for z in DEPTH_ORDER)
LOC_ORDER = (2, 0, 1, 3)
SHARDS = DEPTH * PLANE * 2
PEERS = RUNS * CHUNKS * HEADS_HERE
QN = PEERS * TILE
KN = PEERS * CHUNK
STEP = 256
FLOOR = -1e20
MASKED = -1e30
FAR = 1e6
bf16 = jnp.bfloat16
f32 = jnp.float32


def iota(shape, dim):
    return lax.broadcasted_iota(jnp.int32, shape, dim)


def pick(condition, rows):
    select = jnp.where(condition, f32(1), f32(0)).astype(bf16)
    return jnp.dot(select, rows, preferred_element_type=f32)


def three_parts(x):
    high = x.astype(bf16).astype(f32)
    middle = (x - high).astype(bf16).astype(f32)
    return high, middle, x - high - middle


def exchange(blocks, groups):
    return lax.all_to_all(
        blocks, EVERY, split_axis=0, concat_axis=0, tiled=True, axis_index_groups=groups
    )


def seq_groups(depth_order):
    return [
        [((z * PLANE + spot) * 2 + core) * LOCS + loc for z in depth_order for spot in range(PLANE - 1, -1, -1)]
        for core in range(2)
        for loc in range(LOCS)
    ]


def loc_groups():
    return [[shard * LOCS + loc for loc in LOC_ORDER] for shard in range(SHARDS)]


def start_all(pairs, sems):
    copies = [pltpu.make_async_copy(a, b, sems.at[n]) for n, (a, b) in enumerate(pairs)]
    for copy in copies:
        copy.start()
    return copies


def pack(pos_hbm, q_hbm, k_hbm, v_hbm, out_hbm, pos_ref, q_ref, k_ref, v_ref, out_ref, sems, out_sems):
    copies = start_all([(pos_hbm, pos_ref), (q_hbm, q_ref), (k_hbm, k_ref), (v_hbm, v_ref)], sems)
    for copy in copies[:2]:
        copy.wait()

    wide = (PAD, HEADS_HERE * HEAD_DIM)
    to, source = iota((PAD, ROWS), 0), iota((PAD, ROWS), 1)
    place = to % TILE
    queries = pick((source == to // TILE * RUN + place) & (place < RUN), q_ref[...])
    first = (pos_ref[0] // RUN).astype(f32)
    second = (pos_ref[RUN] // RUN).astype(f32)
    numbers = jnp.where(iota(wide, 1) % HEAD_DIM < HEAD_DIM // 2, first, second)
    queries = jnp.where(iota(wide, 0) % TILE == RUN, numbers, queries).astype(bf16)

    for copy in copies[2:]:
        copy.wait()
    to, source = iota((CHUNKS * TILE, ROWS), 0), iota((CHUNKS * TILE, ROWS), 1)
    place = to % TILE
    row = to // TILE * CHUNK + place % CHUNK
    both = pick((source == row) & (place < CHUNK), k_ref[...])
    both = (both + pick((source == row) & (place >= CHUNK), v_ref[...])).astype(bf16)
    sent = []
    for z in range(RUNS * CHUNKS):
        i, j = z // CHUNKS, z % CHUNKS
        for h in range(HEADS_HERE):
            cols = slice(h * HEAD_DIM, (h + 1) * HEAD_DIM)
            out_ref[z * HEADS_HERE + h, 0:TILE, :] = queries[i * TILE : (i + 1) * TILE, cols]
            out_ref[z * HEADS_HERE + h, TILE : 2 * TILE, :] = both[j * TILE : (j + 1) * TILE, cols]
        mine = pl.ds(z * HEADS_HERE, HEADS_HERE)
        sent.append(pltpu.make_async_copy(out_ref.at[mine], out_hbm.at[mine], out_sems.at[z]))
        sent[-1].start()
    for copy in sent:
        copy.wait()


def pack_embed(e_ref, gain_ref, own_out, first_out, second_out):
    height, rows = LOCS * 2 * PAD, ROWS * PATCH
    to, source = iota((height, rows), 0), iota((height, rows), 1)
    place = to % TILE
    patch = to // TILE % RUNS * RUN + place
    slot = (to // (2 * PAD) ^ lax.axis_index("loc")) * 2 + to // PAD % 2
    moved = pick((source == patch * PATCH + slot) & (place < RUN), e_ref[...])
    high, middle, low = three_parts(gain_ref[...])
    row = iota((height, COLS), 0) % (2 * PAD)
    moved = jnp.where(row == RUN, high, moved)
    moved = jnp.where(row == TILE + RUN, middle, moved)
    moved = jnp.where(row == PAD + RUN, low, moved).astype(bf16)
    step = [moved[n * 2 * PAD : (n + 1) * 2 * PAD, :] for n in range(LOCS)]
    own_out[...] = step[0]
    first_out[0, :, :] = step[3]
    first_out[1, :, :] = step[2]
    second_out[...] = step[1]


def split(in_ref, out_ref):
    both = in_ref[:, TILE : 2 * TILE, :].astype(f32)
    out_ref[0:KN, :] = both[:, 0:CHUNK, :].reshape(KN, HEAD_DIM).astype(bf16)
    out_ref[KN : 2 * KN, :] = both[:, CHUNK:TILE, :].reshape(KN, HEAD_DIM).astype(bf16)
    numbers = in_ref[:, 0:TILE, :].astype(f32)[:, RUN:TILE, :]
    out_ref[2 * KN : 2 * KN + PEERS, :] = numbers.reshape(PEERS, HEAD_DIM).astype(bf16)


def run_starts(numbers):
    other = pltpu.roll(numbers, HEAD_DIM // 2, 1)
    lower = iota(numbers.shape, 1) < HEAD_DIM // 2
    return jnp.where(lower, numbers, other) * RUN, jnp.where(lower, other, numbers) * RUN


def key_positions(numbers, chunk):
    spot = iota((PEERS, KN), 1) // CHUNK == iota((PEERS, KN), 0)
    spot = jnp.where(spot, f32(1), f32(0)).astype(bf16)
    both = lax.dot_general(
        numbers, spot, (((0,), (0,)), ((), ())), preferred_element_type=f32
    )
    half = HEAD_DIM // 2
    first, second = both[0:8, :] * RUN, both[half : half + 8, :] * RUN
    row = iota((8, KN), 1) % CHUNK + chunk * CHUNK
    place = row.astype(f32)
    pos = jnp.where(row < RUN, first + place, second + (place - RUN))
    return jnp.where(row < ROWS, pos, f32(FAR))[0:1, :]


def attend(in_ref, kv_ref, out_hbm, out_ref, s_ref, sems):
    scale = math.log2(math.e) / math.sqrt(HEAD_DIM)
    z = lax.axis_index("za") * 4 + lax.axis_index("zb") * 2 + lax.axis_index("zc")
    place = sum(jnp.where(z == there, n, 0) for n, there in enumerate(DEPTH_ORDER))
    run, chunk = place // CHUNKS, place % CHUNKS
    key_pos, values = [], []
    for core in range(2):
        key_pos.append(key_positions(kv_ref[core, 2 * KN : 2 * KN + PEERS, :], chunk))
        ones = jnp.ones((KN, HEAD_DIM), bf16)
        values.append(jnp.concatenate([kv_ref[core, KN : 2 * KN, :], ones], axis=1))
    numbers = in_ref[:, 0:TILE, :].astype(f32)[:, RUN:TILE, :].reshape(PEERS, HEAD_DIM)
    first, second = run_starts(numbers)
    start = jnp.where(run == 0, first, second)
    blocks = STEP // TILE
    line = iota((blocks, TILE, HEAD_DIM), 1)
    lane = iota((blocks, TILE, HEAD_DIM), 2)
    own = (lane % TILE == line) & (lane < 3 * TILE)
    side = iota((blocks, HEAD_DIM), 1) // TILE
    copies = KN // HEAD_DIM
    sent = []
    for t in range(QN // STEP):
        tile = slice(t * blocks, (t + 1) * blocks)
        queries = in_ref[tile, 0:TILE, :].reshape(STEP, HEAD_DIM)
        pos = jnp.broadcast_to(start[tile, None, :], line.shape) + line.astype(f32)
        pos = jnp.where(line < RUN, pos, f32(-1)).reshape(STEP, HEAD_DIM)
        pos = jnp.concatenate([pos] * copies, axis=1)
        best = jnp.full((STEP, HEAD_DIM), FLOOR, f32)
        for core in range(2):
            scores = lax.dot_general(
                queries, kv_ref[core, 0:KN, :], (((1,), (1,)), ((), ())), preferred_element_type=f32
            )
            scores = jnp.where(key_pos[core] <= pos, scores * scale, f32(MASKED))
            s_ref[core, :, :] = scores
            for n in range(copies):
                best = jnp.maximum(best, scores[:, n * HEAD_DIM : (n + 1) * HEAD_DIM])
        best = jnp.broadcast_to(jnp.max(best, axis=1, keepdims=True), best.shape)
        wide = jnp.concatenate([best] * copies, axis=1)
        acc = jnp.zeros((STEP, 2 * HEAD_DIM), f32)
        for core in range(2):
            weights = jnp.exp2(s_ref[core, :, :] - wide).astype(bf16)
            acc = acc + jnp.dot(weights, values[core], preferred_element_type=f32)
        total = jnp.maximum(acc[:, HEAD_DIM:], f32(1e-30))
        result = (acc[:, 0:HEAD_DIM] / total).reshape(line.shape)
        best = jnp.sum(jnp.where(own, best.reshape(own.shape), f32(0)), axis=1)
        total = jnp.sum(jnp.where(own, total.reshape(own.shape), f32(0)), axis=1)
        level = best + jnp.log(jnp.maximum(total, f32(1e-30))) * math.log2(math.e)
        high, middle, low = three_parts(level)
        level = jnp.where(side == 0, high, jnp.where(side == 1, middle, low))
        level = jnp.where(side < 3, level, f32(0))
        level = jnp.broadcast_to(level[:, None, :], line.shape)
        out_ref[tile, :, :] = jnp.where(line < RUN, result, level).astype(bf16)
        for depth in range(t * blocks // PLANE, (t + 1) * blocks // PLANE):
            mine = out_ref.at[pl.ds(depth * PLANE, PLANE)]
            home = out_hbm.at[pl.ds(HOME_PLACE[depth] * PLANE, PLANE)]
            sent.append(pltpu.make_async_copy(mine, home, sems.at[depth]))
            sent[-1].start()
    for copy in sent:
        copy.wait()


def finish(part_ref, w_ref, own_ref, first_ref, second_ref, out_ref, e_ref):
    arrived = (own_ref[...], second_ref[0, :, :], second_ref[1, :, :], first_ref[0, :, :])
    for step, block in enumerate(arrived):
        origin = lax.axis_index("loc") ^ step
        e_ref[:, pl.ds(pl.multiple_of(origin * COLS, COLS), COLS)] = block
    levels = part_ref[...].astype(f32)[:, RUN:TILE, :].reshape(PEERS, HEAD_DIM)
    levels = levels + pltpu.roll(levels, 128 - TILE, 1) + pltpu.roll(levels, 128 - 2 * TILE, 1)
    levels = jnp.concatenate(
        [levels[at * PLANE : (at + 1) * PLANE, :] for at in HOME_PLACE], axis=0
    ).reshape(RUNS, CHUNKS, HEADS_HERE, 128)
    levels = jnp.exp2(levels - jnp.max(levels, axis=1, keepdims=True))
    shares = levels / jnp.sum(levels, axis=1, keepdims=True)
    shares = jnp.concatenate(
        [shares.reshape(PEERS, 128), jnp.zeros((128 - PEERS, 128), f32)], axis=0
    ).T
    real = iota((TILE, HEAD_DIM), 0) < RUN
    per_slot = SLOT_D // HEAD_DIM
    rows = []
    for u in range(2):
        for i in range(RUNS):
            heads = []
            for h in range(u * per_slot, (u + 1) * per_slot):
                acc = jnp.zeros((TILE, HEAD_DIM), f32)
                for j in range(CHUNKS):
                    block = (i * CHUNKS + j) * HEADS_HERE + h
                    partial = part_ref[HOME_PLACE[block // PLANE] * PLANE + h, :, :].astype(f32)
                    acc = acc + shares[0:TILE, block : block + 1] * partial
                heads.append(jnp.where(real, acc, f32(0)).astype(bf16))
            rows.append(jnp.concatenate(heads, axis=1))
    slots = jnp.concatenate(rows, axis=0)
    embed = e_ref[...].astype(f32)
    gain = embed[RUN : RUN + 1, :] + embed[TILE + RUN : TILE + RUN + 1, :] + embed[PAD + RUN : PAD + RUN + 1, :]
    mixed = jnp.dot(slots, w_ref[...], preferred_element_type=f32) + embed
    spread = jnp.sum(mixed * mixed, axis=1, keepdims=True) / LOCAL_D + 1e-05
    normed = (mixed / jnp.sqrt(spread) * gain).astype(bf16)
    for part in range(LOCS):
        out_ref[LOC_ORDER.index(part), :, :] = normed[:, part * COLS : (part + 1) * COLS]


def unpack(in_ref, out_ref):
    height, rows = LOCS * 2 * PAD, ROWS * PATCH
    to, source = iota((rows, height), 0), iota((rows, height), 1)
    patch = to // PATCH
    row = to % PATCH * PAD + patch // RUN * TILE + patch % RUN
    arrived = jnp.concatenate([in_ref[LOC_ORDER.index(loc), :, :] for loc in range(LOCS)], axis=0)
    moved = pick(source == row, arrived)
    out_ref[...] = moved.astype(bf16)


def vmem(count):
    return [pl.BlockSpec(memory_space=pltpu.VMEM)] * count


def call(kernel, outs, specs, scratch=(), flops=0, moved=0, limit=40 * 1024 * 1024, to_hbm=False):
    space = pltpu.HBM if to_hbm else pltpu.VMEM
    return pl.pallas_call(
        kernel,
        out_shape=outs,
        in_specs=specs,
        out_specs=jax.tree.map(lambda _: pl.BlockSpec(memory_space=space), outs),
        scratch_shapes=scratch,
        compiler_params=pltpu.CompilerParams(vmem_limit_bytes=limit),
        cost_estimate=pl.CostEstimate(flops=flops, bytes_accessed=moved, transcendentals=0),
        name=kernel.__name__,
    )


def shape(*dims):
    return jax.ShapeDtypeStruct(dims, bf16)


def swapped(block, step):
    return lax.ppermute(block, "loc", [(i, i ^ step) for i in range(LOCS)])


def on_device(queries, keys, values, positions, byte_embed, w_slot, gain):
    wide = (ROWS, HEADS_HERE * HEAD_DIM)
    messages = (PEERS, 2 * TILE, HEAD_DIM)
    results = (PEERS, TILE, HEAD_DIM)
    sent = call(
        pack,
        shape(*messages),
        [pl.BlockSpec(memory_space=pltpu.HBM)] * 4,
        [
            pltpu.SMEM((ROWS,), jnp.int32),
            pltpu.VMEM(wide, bf16),
            pltpu.VMEM(wide, bf16),
            pltpu.VMEM(wide, bf16),
            pltpu.VMEM(messages, bf16),
            pltpu.SemaphoreType.DMA((4,)),
            pltpu.SemaphoreType.DMA((RUNS * CHUNKS,)),
        ],
        limit=None,
        to_hbm=True,
    )(positions, queries, keys, values)
    sent, byte_embed = lax.optimization_barrier((sent, byte_embed))
    held = exchange(sent, seq_groups(DEPTH_ORDER))
    own, first, second = call(
        pack_embed,
        [shape(2 * PAD, COLS), shape(2, 2 * PAD, COLS), shape(2 * PAD, COLS)],
        vmem(2),
    )(byte_embed, gain.reshape(1, COLS))
    held, first = lax.optimization_barrier((held, swapped(first, 3)))
    kv = call(split, shape(2 * KN + PEERS, HEAD_DIM), vmem(1))(held)
    kv = lax.all_gather(kv, "c", axis=0, tiled=False)
    partial = call(
        attend,
        shape(*results),
        vmem(2),
        [
            pltpu.VMEM(results, bf16),
            pltpu.VMEM((2, STEP, KN), f32),
            pltpu.SemaphoreType.DMA((DEPTH,)),
        ],
        flops=4 * QN * 2 * KN * HEAD_DIM,
        moved=2 * 4 * KN * HEAD_DIM,
        to_hbm=True,
    )(held, kv)
    partial, first, second = lax.optimization_barrier((partial, first, second))
    second = swapped(jnp.stack([second, first[1]]), 1)
    partial = exchange(partial, seq_groups(HOME_ORDER))
    normed = call(
        finish,
        shape(LOCS, 2 * PAD, COLS),
        vmem(5),
        [pltpu.VMEM((2 * PAD, LOCAL_D), bf16)],
    )(partial, w_slot, own, first, second)
    columns = exchange(normed, loc_groups())
    return call(unpack, shape(ROWS * PATCH, COLS), vmem(1))(columns)


def solution(mesh):
    devices = mesh.devices.reshape(2, 2, 2, 4, 2, 2, LOCS)
    finer = Mesh(devices, SEQ + ("loc",))
    placed = (
        P(SEQ, "loc"),
        P(SEQ, "loc"),
        P(SEQ, "loc"),
        P(SEQ),
        P(SEQ, "loc"),
        P(),
        P("loc"),
    )
    return jax.shard_map(
        on_device, mesh=finer, in_specs=placed, out_specs=P(SEQ, "loc"), check_vma=False
    )
```
